128 devices in a mesh: seq: 2 (over z_hi), head: 2 (over z_lo), blk: 32 (over y, x, core).
Axes of the slice: x: 4, y: 4, z: 4 (z_hi: 2, z_lo: 2; z = z_hi * 2 + z_lo), core: 2. Of those that a mesh axis runs over, the one named last changes fastest.
Arguments:
- inputs: bfloat16 [2, 8192, 1024], P('seq', ('blk', 'head')), may hold values from -6 to 6
- w_query: bfloat16 [1024, 2048], P(('seq', 'head', 'blk')), may hold values from -0.1875 to 0.1875
- key_weight: bfloat16 [1024, 1024], P(('seq', 'head', 'blk')), may hold values from -0.1875 to 0.1875
- value_weight: bfloat16 [1024, 1024], P(('seq', 'head', 'blk')), may hold values from -0.1875 to 0.1875
- w_output: bfloat16 [2048, 1024], P(('seq', 'head', 'blk')), may hold values from -6 to 6
- w_gate: bfloat16 [1024, 3072], P(('seq', 'head', 'blk')), may hold values from -0.1875 to 0.1875
- w_up: bfloat16 [1024, 3072], P(('seq', 'head', 'blk')), may hold values from -0.1875 to 0.1875
- w_down: bfloat16 [3072, 1024], P(('seq', 'head', 'blk')), may hold values from -0.109375 to 0.109375
- gain_attn: float32 [1024], replicated, may hold values from 0.5 to 1.5
- gain_ffn: float32 [1024], replicated, may hold values from 0.5 to 1.5
- gain_query: float32 [128], replicated, may hold values from 0.5 to 1.5
- gain_key: float32 [128], replicated, may hold values from 0.5 to 1.5
- grad_outputs: bfloat16 [2, 8192, 1024], P('seq', ('blk', 'head')), may hold values from -6 to 6
Outputs:
- result: bfloat16 [2, 8192, 1024], P('seq', ('blk', 'head'))
- grad_inputs: bfloat16 [2, 8192, 1024], P('seq', ('blk', 'head'))
- grad_w_query: float32 [1024, 2048], P(('seq', 'head', 'blk'))
- grad_w_key: float32 [1024, 1024], P(('seq', 'head', 'blk'))
- grad_w_value: float32 [1024, 1024], P(('seq', 'head', 'blk'))
- grad_w_output: float32 [2048, 1024], P(('seq', 'head', 'blk'))
- grad_w_gate: float32 [1024, 3072], P(('seq', 'head', 'blk'))
- grad_w_up: float32 [1024, 3072], P(('seq', 'head', 'blk'))
- grad_w_down: float32 [3072, 1024], P(('seq', 'head', 'blk'))
- grad_gain_attn: float32 [1024], replicated
- grad_gain_ffn: float32 [1024], replicated
- grad_gain_query: float32 [128], replicated
- grad_gain_key: float32 [128], replicated
The draws below stay inside these ranges and needn't reach their ends.
All inputs are finite; a program needn't handle non-finite values.
Results may differ from the reference program's by a relative error of at most 0.024.
Values may be sent and summed in bfloat16 or wider, within the bound.
No kernel may reach another device: no remote copies, remote signals or barrier semaphores. Data moves between devices by JAX's collectives and lax.ppermute only.
A program may use at most 256 MiB of HBM per device.

```python
import jax
import jax.numpy as jnp
from jax import lax

MODEL_WIDTH = 1024
HQ = 16
VALUE_KEY_HEADS = 8
HEAD_SIZE = 128
FF = 3072
SEQ_LEN = 8192
SEQS = 2


def level_of(own_key, dims, cuts, least, high):
    level = 1.0
    for axis_at, blocks in cuts:
        steps = jax.random.uniform(jax.random.fold_in(jax.random.fold_in(own_key, 6), axis_at), (blocks,), jnp.float32, least / len(cuts), high / len(cuts))
        level = level * jnp.repeat(jnp.exp(steps), dims[axis_at] // blocks).reshape((-1,) + (1,) * (len(dims) - 1 - axis_at))
    return level


def centred(own_key, shape, deviation, limit, shards=(), kind=jnp.bfloat16):
    array = deviation * jax.random.normal(own_key, shape, jnp.float32)
    if shards:
        array = array * level_of(own_key, shape, shards, -0.22, 0.18)
    return jnp.clip(array, -limit, limit).astype(kind)


def setup_inputs(seed: int = 0) -> dict:
    key_list = jax.random.split(jax.random.key(seed), 14)
    return {
        "inputs": centred(key_list[0], (SEQS, SEQ_LEN, MODEL_WIDTH), 1.0, 6.0, ((0, 2), (1, 64))),
        "w_query": centred(key_list[1], (MODEL_WIDTH, HQ * HEAD_SIZE), MODEL_WIDTH ** -0.5, 0.1875, ((0, 128),)),
        "key_weight": centred(key_list[2], (MODEL_WIDTH, VALUE_KEY_HEADS * HEAD_SIZE), MODEL_WIDTH ** -0.5, 0.1875, ((0, 128),)),
        "value_weight": centred(key_list[3], (MODEL_WIDTH, VALUE_KEY_HEADS * HEAD_SIZE), MODEL_WIDTH ** -0.5, 0.1875, ((0, 128),)),
        "w_output": centred(key_list[4], (HQ * HEAD_SIZE, MODEL_WIDTH), (max(1, HQ * HEAD_SIZE * 4 // SEQ_LEN)) ** -0.5, 6.0, ((0, 128),)),
        "w_gate": centred(key_list[5], (MODEL_WIDTH, FF), MODEL_WIDTH ** -0.5, 0.1875, ((0, 128),)),
        "w_up": centred(key_list[6], (MODEL_WIDTH, FF), MODEL_WIDTH ** -0.5, 0.1875, ((0, 128),)),
        "w_down": centred(key_list[7], (FF, MODEL_WIDTH), FF ** -0.5, 0.109375, ((0, 128),)),
        "gain_attn": jnp.clip(1.0 + 0.1 * jax.random.normal(key_list[8], (MODEL_WIDTH,), jnp.float32), 0.5, 1.5),
        "gain_ffn": jnp.clip(1.0 + 0.1 * jax.random.normal(key_list[9], (MODEL_WIDTH,), jnp.float32), 0.5, 1.5),
        "gain_query": jnp.clip(1.0 + 0.1 * jax.random.normal(key_list[10], (HEAD_SIZE,), jnp.float32), 0.5, 1.5),
        "gain_key": jnp.clip(1.0 + 0.1 * jax.random.normal(key_list[11], (HEAD_SIZE,), jnp.float32), 0.5, 1.5),
        "grad_outputs": centred(key_list[12], (SEQS, SEQ_LEN, MODEL_WIDTH), 1.0, 6.0, ((0, 2), (1, 64))),
    }


epsilon = 1e-06
rope_base = 1000000.0
masked_value = -1e+30

@jax.custom_vjp
def low(v):
    return lax.optimization_barrier(v.astype(jnp.bfloat16)).astype(jnp.float32)

@jax.custom_vjp
def low_back(v):
    return v

def low_keep(v):
    return (low(v), None)

def low_pass(kept, grad):
    return (grad,)

def back_keep(v):
    return (v, None)

def back_low(kept, grad):
    return (low(grad),)
low.defvjp(low_keep, low_pass)
low_back.defvjp(back_keep, back_low)

def rms_scale(values, gain):
    return values * lax.rsqrt(lax.optimization_barrier(jnp.mean(values * values, axis=-1, keepdims=True)) + epsilon) * gain

def rotate(values, cosine, sine):
    half = values.shape[-1] // 2
    first = values[..., :half]
    second_result = values[..., half:]
    return jnp.concatenate([first * cosine - second_result * sine, second_result * cosine + first * sine], axis=-1)

def rope_tables(length, width):
    freqs = rope_base ** (-(jnp.arange(width // 2, dtype=jnp.float32) * 2.0 / width))
    angles = jnp.arange(length, dtype=jnp.int32).astype(jnp.float32)[:, None] * freqs[None, :]
    return (jnp.cos(angles)[:, None, :], jnp.sin(angles)[:, None, :])

def attend(queries, keys, values):
    length, heads, width = queries.shape
    kv_heads = keys.shape[1]
    block = 512 if length % 512 == 0 else length
    grouped = queries.reshape(length // block, block, kv_heads, heads // kv_heads, width)
    starts = jnp.arange(length // block, dtype=jnp.int32) * block
    key_rows = jnp.arange(length, dtype=jnp.int32)

    @jax.checkpoint
    def one_block(pair):
        part, begin = pair
        scores = low_back(jnp.einsum('qhgd,khd->qhgk', part, keys, precision=lax.Precision.HIGHEST))
        rows = begin + jnp.arange(block, dtype=jnp.int32)
        allowed = (key_rows[None, :] <= rows[:, None])[:, None, None, :]
        scores = jnp.where(allowed, scores, masked_value)
        probs = jax.nn.softmax(scores, axis=-1)
        return jnp.einsum('qhgk,khd->qhgd', low(probs), values, precision=lax.Precision.HIGHEST)
    output = lax.map(one_block, (grouped, starts))
    return output.reshape(length, heads, width)

def forward(inputs, w_query, key_weight, value_weight, w_output, w_gate, w_up, w_down, gain_attn, gain_ffn, gain_query, gain_key):
    seqs, length, width = inputs.shape
    head_dim = gain_query.shape[0]
    cosine, sine = rope_tables(length, head_dim)
    highest = lax.Precision.HIGHEST
    hidden_one = low(rms_scale(inputs, gain_attn))
    q_raw = low_back(jnp.matmul(hidden_one, w_query, precision=highest)).reshape(seqs, length, -1, head_dim)
    k_raw = low_back(jnp.matmul(hidden_one, key_weight, precision=highest)).reshape(seqs, length, -1, head_dim)
    values = low_back(low(jnp.matmul(hidden_one, value_weight, precision=highest))).reshape(seqs, length, -1, head_dim)
    queries = low_back(low(rotate(rms_scale(q_raw, gain_query), cosine, sine) * head_dim ** (-0.5)))
    keys = low_back(low(rotate(rms_scale(k_raw, gain_key), cosine, sine)))
    attended = jnp.stack([attend(queries[index], keys[index], values[index]) for index in range(seqs)])
    attended = low_back(low(attended.reshape(seqs, length, -1)))
    mid = inputs + low_back(jnp.matmul(attended, w_output, precision=highest))
    hidden_after_attention = low(rms_scale(mid, gain_ffn))
    gate = low_back(jnp.matmul(hidden_after_attention, w_gate, precision=highest))
    up = low_back(jnp.matmul(hidden_after_attention, w_up, precision=highest))
    act = low(jax.nn.silu(gate) * up)
    return mid + low_back(jnp.matmul(act, w_down, precision=highest))

def reference(inputs, w_query, key_weight, value_weight, w_output, w_gate, w_up, w_down, gain_attn, gain_ffn, gain_query, gain_key, grad_outputs):
    operands = [value.astype(jnp.float32) for value in (inputs, w_query, key_weight, value_weight, w_output, w_gate, w_up, w_down, gain_attn, gain_ffn, gain_query, gain_key)]
    result, pull = jax.vjp(forward, *operands)
    grads = pull(grad_outputs.astype(jnp.float32))
    return (result.astype(jnp.bfloat16), grads[0].astype(jnp.bfloat16), grads[1], grads[2], grads[3], grads[4], grads[5], grads[6], grads[7], grads[8], grads[9], grads[10], grads[11])
```

```python
import functools

import jax
import jax.numpy as jnp
from jax import lax
from jax.experimental import pallas as pl
from jax.experimental.pallas import tpu as pltpu
from jax.sharding import Mesh, PartitionSpec as P

EPS = 1e-06
ROPE_BASE = 1000000.0
BF = jnp.bfloat16
F32 = jnp.float32
HD = 128
ALL = ("seq", "head", "y", "x", "core")
Z = ("seq", "head")
VMEM = pl.BlockSpec(memory_space=pltpu.VMEM)
SMEM = pl.BlockSpec(memory_space=pltpu.SMEM)
PARAMS = pltpu.CompilerParams(vmem_limit_bytes=48 * 1024 * 1024)


def swap(v, axis, m):
    n = 2 if axis == "core" or axis == "head" else 4
    return lax.ppermute(v, axis, [(i, i ^ m) for i in range(n)])


def pick4(parts, me):
    b0 = (me & 1) == 1
    b1 = (me & 2) == 2
    return [
        jnp.where(b1, jnp.where(b0, parts[k ^ 3], parts[k ^ 2]), jnp.where(b0, parts[k ^ 1], parts[k]))
        for k in range(4)
    ]


def gather_group(v):
    w = jnp.stack([v] + [swap(v, "y", d) for d in (1, 2, 3)])
    return jnp.stack([w, swap(w, "core", 1)], axis=1)


def scatter_group(part):
    s = part[:, 0] + swap(part[:, 1].astype(BF), "core", 1).astype(F32)
    sb = s.astype(BF)
    got = [swap(sb[d], "y", d).astype(F32) for d in (1, 3, 2)]
    return s[0] + got[0] + got[1] + got[2]


def exchange_group(v):
    w = jnp.stack([v[:, 0], swap(v[:, 1], "core", 1)], axis=1)
    r = {d: swap(w[d], "y", d) for d in (1, 3, 2)}
    return jnp.stack([w[0], r[1], r[2], r[3]])


def gather_x(v, me, axis):
    return jnp.stack(pick4([v] + [swap(v, "x", d) for d in (1, 2, 3)], me), axis=axis)


def gather_z(v, me):
    return jnp.stack(pick4([v] + [swap(v, Z, d) for d in (1, 2, 3)], me), axis=0)


def reduce_slots(parts, axis, me):
    parts = pick4(parts, me)
    total = parts[0]
    for d in (1, 3, 2):
        total = total + swap(parts[d].astype(BF), axis, d).astype(F32)
    return total


def qkv_kernel(x_ref, gain_ref, w_ref, gq_ref, gk_ref, cos_ref, sin_ref, h_ref, q_ref, kv_ref, raw_ref):
    x = x_ref[...].astype(F32)
    scale = lax.rsqrt(jnp.mean(x * x, axis=-1, keepdims=True) + EPS)
    h = (x * scale * gain_ref[...]).astype(BF)
    h_ref[...] = h
    raw = jnp.dot(h, w_ref[...], preferred_element_type=F32)
    raw_ref[...] = raw[:, : 3 * HD]
    cos = cos_ref[...]
    sin = sin_ref[...]

    def shaped(v, gain, factor):
        r = lax.rsqrt(jnp.mean(v * v, axis=-1, keepdims=True) + EPS)
        u = v * r * gain
        return ((u * cos + pltpu.roll(u, HD // 2, 1) * sin) * factor).astype(BF)

    factor = HD ** (-0.5)
    q_ref[:, :HD] = shaped(raw[:, :HD], gq_ref[...], factor)
    q_ref[:, HD:] = shaped(raw[:, HD : 2 * HD], gq_ref[...], factor)
    kv_ref[:, :HD] = shaped(raw[:, 2 * HD : 3 * HD], gk_ref[...], 1.0)
    kv_ref[:, HD:] = raw[:, 3 * HD :].astype(BF)


def qkv_project(x, gain, w, gq, gk, cos, sin):
    rows, width = x.shape
    tile = 256
    row = lambda n: pl.BlockSpec((tile, n), lambda i: (i, 0))
    whole = lambda a: pl.BlockSpec(a.shape, lambda i: (0, 0))
    return pl.pallas_call(
        qkv_kernel,
        grid=(rows // tile,),
        in_specs=[row(width), whole(gain), whole(w), whole(gq), whole(gk), row(HD), row(HD)],
        out_specs=[row(width), row(2 * HD), row(2 * HD), row(3 * HD)],
        out_shape=[
            jax.ShapeDtypeStruct((rows, width), BF),
            jax.ShapeDtypeStruct((rows, 2 * HD), BF),
            jax.ShapeDtypeStruct((rows, 2 * HD), BF),
            jax.ShapeDtypeStruct((rows, 3 * HD), F32),
        ],
        compiler_params=PARAMS,
        cost_estimate=pl.CostEstimate(flops=2 * rows * width * 512, bytes_accessed=8 << 20, transcendentals=0),
        name="qkv_project",
    )(x, gain, w, gq, gk, cos, sin)


def qkv_back_kernel(dq_ref, dkv_ref, raw_ref, gq_ref, gk_ref, cos_ref, sin_ref, out_ref, gain_ref):
    cos = cos_ref[...]
    sin = sin_ref[...]

    @pl.when(pl.program_id(0) == 0)
    def _():
        gain_ref[...] = jnp.zeros_like(gain_ref)

    def back(d, v, gain, factor):
        d = d.astype(F32) * factor
        d = d * cos + pltpu.roll(d * sin, HD // 2, 1)
        r = lax.rsqrt(jnp.mean(v * v, axis=-1, keepdims=True) + EPS)
        u = v * r
        t = d * gain
        raw = r * (t - u * jnp.mean(t * u, axis=-1, keepdims=True))
        return raw.astype(BF), jnp.sum(d * u, axis=0, keepdims=True)

    factor = HD ** (-0.5)
    a, ga = back(dq_ref[:, :HD], raw_ref[:, :HD], gq_ref[...], factor)
    b, gb = back(dq_ref[:, HD:], raw_ref[:, HD : 2 * HD], gq_ref[...], factor)
    c, gc = back(dkv_ref[:, :HD], raw_ref[:, 2 * HD :], gk_ref[...], 1.0)
    out_ref[:, :HD] = a
    out_ref[:, HD : 2 * HD] = b
    out_ref[:, 2 * HD : 3 * HD] = c
    out_ref[:, 3 * HD :] = dkv_ref[:, HD:]
    gain_ref[0:1, :] += ga + gb
    gain_ref[1:2, :] += gc


def qkv_back(dq, dkv, raw, gq, gk, cos, sin):
    rows = dq.shape[0]
    tile = 256
    row = lambda n: pl.BlockSpec((tile, n), lambda i: (i, 0))
    whole = lambda a: pl.BlockSpec(a.shape, lambda i: (0, 0))
    return pl.pallas_call(
        qkv_back_kernel,
        grid=(rows // tile,),
        in_specs=[row(2 * HD), row(2 * HD), row(3 * HD), whole(gq), whole(gk), row(HD), row(HD)],
        out_specs=[row(4 * HD), pl.BlockSpec((8, HD), lambda i: (0, 0))],
        out_shape=[jax.ShapeDtypeStruct((rows, 4 * HD), BF), jax.ShapeDtypeStruct((8, HD), F32)],
        compiler_params=PARAMS,
        name="qkv_back",
    )(dq, dkv, raw, gq, gk, cos, sin)


TILE = 256


def pair_of(i):
    t = jnp.where(i < 1, 1, jnp.where(i < 3, 2, 3))
    u = jnp.where(i < 1, 0, jnp.where(i < 3, i - 1, i - 3))
    return t, u


def spread(core, key_axis):
    shape = (TILE, TILE)
    a = lax.broadcasted_iota(jnp.int32, shape, key_axis)
    b = lax.broadcasted_iota(jnp.int32, shape, 1 - key_axis)
    flip = core * 128

    def place(i):
        j = i ^ flip
        return j + (j & 128)

    return place(a) - place(b)


def attend_kernel(first, last, deltas, meta_ref, *refs):
    n = len(deltas)
    q_ref = refs[0]
    kv_refs = refs[1 : 1 + n]
    at = 1 + n
    if not first:
        acc_in, sum_in = refs[at : at + 2]
        at += 2
    if last:
        att_ref, low_ref, sum_ref = refs[at : at + 3]
        acc_ref, mask_ref = refs[at + 3 :]
    else:
        acc_ref, sum_ref = refs[at : at + 2]
        (mask_ref,) = refs[at + 2 :]
    if first:
        acc_ref[...] = jnp.zeros_like(acc_ref)
        sum_ref[...] = jnp.zeros_like(sum_ref)
    else:
        acc_ref[...] = acc_in[...]
        sum_ref[...] = sum_in[...]
    y, core, x, head = meta_ref[0], meta_ref[1], meta_ref[2], meta_ref[3]
    mask_ref[...] = spread(core, 1)

    def unit(kv_ref, t, u, limit):
        rows = pl.ds(pl.multiple_of((t ^ y) * TILE, TILE), TILE)
        cols = pl.ds(pl.multiple_of((u ^ y) * TILE, TILE), TILE)
        key = kv_ref[cols, :HD]
        value = kv_ref[cols, HD:]
        for h in range(2):
            lanes = slice(h * HD, (h + 1) * HD)
            s = lax.dot_general(q_ref[rows, lanes], key, (((1,), (1,)), ((), ())), preferred_element_type=F32)
            p = jnp.exp(s)
            if limit is not None:
                p = jnp.where(mask_ref[...] <= limit, p, 0.0)
            sum_ref[rows, lanes] += p[:, :HD] + p[:, HD:]
            acc_ref[rows, lanes] += jnp.dot(p.astype(BF), value, preferred_element_type=F32)

    for (dx, dh), kv_ref in zip(deltas, kv_refs):
        base = ((x - (x ^ dx)) * 4 + head - (head ^ dh)) * 128

        @pl.loop(0, 6)
        def _(i):
            t, u = pair_of(i)
            unit(kv_ref, t, u, None)

        @pl.loop(0, 4)
        def _(t):
            unit(kv_ref, t, t, base)

    if last:

        @pl.loop(0, 4)
        def _(t):
            rows = pl.ds(pl.multiple_of(t * TILE, TILE), TILE)
            for h in range(2):
                lanes = slice(h * HD, (h + 1) * HD)
                total = jnp.sum(sum_ref[rows, lanes], axis=-1, keepdims=True)
                out = acc_ref[rows, lanes] / total
                att_ref[rows, lanes] = out
                low_ref[rows, lanes] = out.astype(BF)


def attend(meta, q, chunks, deltas, carry, last):
    first = carry is None
    rows = q.shape[0]
    f32 = jax.ShapeDtypeStruct((rows, 2 * HD), F32)
    low = jax.ShapeDtypeStruct((rows, 2 * HD), BF)
    scratch = [pltpu.VMEM((TILE, TILE), jnp.int32)]
    if last:
        scratch = [pltpu.VMEM((rows, 2 * HD), F32)] + scratch
    args = [meta, q, *chunks] + ([] if first else list(carry))
    work = len(deltas) * 10 * 512 * 256
    return pl.pallas_call(
        functools.partial(attend_kernel, first, last, deltas),
        in_specs=[SMEM] + [VMEM] * (len(args) - 1),
        out_specs=[VMEM] * (3 if last else 2),
        out_shape=[f32, low, f32] if last else [f32, f32],
        scratch_shapes=scratch,
        compiler_params=PARAMS,
        cost_estimate=pl.CostEstimate(flops=work * 512, bytes_accessed=6 << 20, transcendentals=work),
        name="attend",
    )(*args)


def attend_back_kernel(first, deltas, meta_ref, *refs):
    n = len(deltas)
    q_ref, do_ref, lse_ref, delta_ref = refs[:4]
    kv_refs = refs[4 : 4 + n]
    at = 4 + n
    if not first:
        dq_in = refs[at]
        at += 1
    dq_ref = refs[at]
    dkv_refs = refs[at + 1 : at + 1 + n]
    acc_ref, mask_ref = refs[at + 1 + n :]
    if first:
        dq_ref[...] = jnp.zeros_like(dq_ref)
    else:
        dq_ref[...] = dq_in[...]
    y, core, x, head = meta_ref[0], meta_ref[1], meta_ref[2], meta_ref[3]
    mask_ref[...] = spread(core, 0)
    nt = (((1,), (1,)), ((), ()))
    tn = (((0,), (0,)), ((), ()))

    def unit(kv_ref, t, u, limit):
        at_q = t ^ y
        rows = pl.ds(pl.multiple_of(at_q * TILE, TILE), TILE)
        cols = pl.ds(pl.multiple_of((u ^ y) * TILE, TILE), TILE)
        key = kv_ref[cols, :HD]
        value = kv_ref[cols, HD:]
        dk = dv = None
        for h in range(2):
            lanes = slice(h * HD, (h + 1) * HD)
            q = q_ref[rows, lanes]
            do = do_ref[rows, lanes]
            s = lax.dot_general(key, q, nt, preferred_element_type=F32)
            p = jnp.exp(s - lse_ref[at_q, h : h + 1, :])
            if limit is not None:
                p = jnp.where(mask_ref[...] <= limit, p, 0.0)
            dp = lax.dot_general(value, do, nt, preferred_element_type=F32)
            ds = (p * (dp - delta_ref[at_q, h : h + 1, :])).astype(BF)
            dv_h = jnp.dot(p.astype(BF), do, preferred_element_type=F32)
            dk_h = jnp.dot(ds, q, preferred_element_type=F32)
            dv = dv_h if dv is None else dv + dv_h
            dk = dk_h if dk is None else dk + dk_h
            dq_ref[rows, lanes] += lax.dot_general(ds, key, tn, preferred_element_type=F32)
        return cols, dk, dv

    for (dx, dh), kv_ref, dkv_ref in zip(deltas, kv_refs, dkv_refs):
        base = ((x - (x ^ dx)) * 4 + head - (head ^ dh)) * 128

        @pl.loop(0, 4)
        def _(t):
            cols, dk, dv = unit(kv_ref, t, t, base)
            acc_ref[cols, :HD] = dk
            acc_ref[cols, HD:] = dv

        @pl.loop(0, 6)
        def _(i):
            t, u = pair_of(i)
            cols, dk, dv = unit(kv_ref, t, u, None)
            acc_ref[cols, :HD] += dk
            acc_ref[cols, HD:] += dv

        dkv_ref[...] = acc_ref[...].astype(BF)


def attend_back(meta, q, do, lse, delta, chunks, deltas, carry):
    first = carry is None
    rows = q.shape[0]
    args = [meta, q, do, lse, delta, *chunks] + ([] if first else [carry])
    n = len(deltas)
    work = n * 10 * 512 * 256
    return pl.pallas_call(
        functools.partial(attend_back_kernel, first, deltas),
        in_specs=[SMEM] + [VMEM] * (len(args) - 1),
        out_specs=[VMEM] * (1 + n),
        out_shape=[jax.ShapeDtypeStruct((rows, 2 * HD), F32)] + [jax.ShapeDtypeStruct((rows, 2 * HD), BF)] * n,
        scratch_shapes=[pltpu.VMEM((rows, 2 * HD), F32), pltpu.VMEM((TILE, TILE), jnp.int32)],
        compiler_params=PARAMS,
        cost_estimate=pl.CostEstimate(flops=work * 1280, bytes_accessed=6 << 20, transcendentals=work),
        name="attend_back",
    )(*args)


def rms_parts(v):
    scale = lax.rsqrt(jnp.mean(v * v, axis=-1, keepdims=True) + EPS)
    return v * scale, scale


def rms_back(unit, scale, gain, grad):
    t = grad * gain
    return scale * (t - unit * jnp.mean(t * unit, axis=-1, keepdims=True))


def local(
    inputs, w_query, key_weight, value_weight, w_output, w_gate, w_up, w_down,
    gain_attn, gain_ffn, gain_query, gain_key, grad_outputs,
):
    sq, hd = lax.axis_index("seq"), lax.axis_index("head")
    y, x, core = lax.axis_index("y"), lax.axis_index("x"), lax.axis_index("core")
    zi = sq * 2 + hd
    tokens = inputs[0]
    count, width = tokens.shape
    rows = 8 * count
    meta = jnp.stack([y, core, x, hd]).astype(jnp.int32)

    slot = jnp.arange(8, dtype=jnp.int32)
    chunk = ((slot // 2) ^ y) * 16 + x * 4 + ((slot % 2) ^ core) * 2 + hd
    pos = (chunk[:, None] * count + jnp.arange(count, dtype=jnp.int32)[None, :]).reshape(-1)
    freqs = ROPE_BASE ** (-(jnp.arange(HD // 2, dtype=F32) * 2.0 / HD))
    angles = pos.astype(F32)[:, None] * freqs[None, :]
    cos, sin = jnp.cos(angles), jnp.sin(angles)
    cos = jnp.concatenate([cos, cos], axis=1)
    sin = jnp.concatenate([-sin, sin], axis=1)

    xg = gather_group(tokens).reshape(rows, width)

    def cut(w):
        return w.reshape(w.shape[0], 8, -1)

    cols = jnp.concatenate([cut(w_query), cut(key_weight), cut(value_weight), cut(w_gate), cut(w_up)], axis=2)
    cols = cols.transpose(1, 0, 2)
    cols = lax.all_to_all(cols, ("y", "core"), split_axis=0, concat_axis=0, tiled=True)
    n_qkv = 4 * HD
    n_ff = w_gate.shape[1] // 8

    def gather_rows(w):
        c = w.shape[-1]
        w = gather_x(w.reshape(4, 16, c), x, 1).reshape(256, c)
        return gather_z(w, zi).reshape(width, c)

    w_qkv = gather_rows(cols[:, :, :n_qkv])

    def index(s, h, yy, xx, c):
        return (((s * 2 + h) * 4 + yy) * 4 + xx) * 2 + c

    there = []
    for s in range(2):
        for h in range(2):
            for yy in range(4):
                for xx in range(4):
                    for c in range(2):
                        to = index(yy % 2, xx // 2, s * 2 + h, (xx % 2) * 2 + c, yy // 2)
                        there.append((index(s, h, yy, xx, c), to))
    back = [(b, a) for a, b in there]
    n_out = w_output.shape[0]
    tall = lax.ppermute(jnp.concatenate([w_output, w_down], axis=0), ALL, there)

    hidden, q, kv, raw = qkv_project(
        xg, gain_attn[None], w_qkv, gain_query[None], gain_key[None], cos, sin
    )

    kv_z = swap(kv, "head", 1)
    kvs = {(0, 0): kv, (0, 1): kv_z}
    for d in (1, 3, 2):
        kvs[(d, 0)] = swap(kv, "x", d)
    for d in (1, 3, 2):
        kvs[(d, 1)] = swap(kv_z, "x", d)

    w_gu = gather_rows(cols[:, :, n_qkv:])
    tall = gather_z(gather_x(tall, x, 0), zi)
    w_out = tall[:, :, :n_out].reshape(16 * n_out, width)
    w_dn = tall[:, :, n_out:].reshape(-1, width)
    w_out_all = gather_group(w_out).reshape(-1, width)
    dyg = gather_group(grad_outputs[0]).reshape(rows, width)

    carry = None
    orders = [((0, 0), (0, 1)), ((1, 0), (3, 0)), ((2, 0), (1, 1)), ((3, 1), (2, 1))]
    for step, deltas in enumerate(orders):
        carry = attend(meta, q, [kvs[d] for d in deltas], deltas, carry, step == len(orders) - 1)
    attended, attended_low, sums = carry
    lse = jnp.log(jnp.sum(sums.reshape(4, TILE, 2, HD), axis=-1)).transpose(0, 2, 1)

    own = exchange_group(attended_low.reshape(4, 2, count, 2 * HD))
    own = own.transpose(2, 0, 1, 3).reshape(count, -1)
    mid = tokens.astype(F32) + jnp.dot(own, w_out_all, preferred_element_type=F32)
    mid_unit, mid_scale = rms_parts(mid)
    h2 = (mid_unit * gain_ffn).astype(BF)
    h2g = gather_group(h2).reshape(rows, width)

    gu = jnp.dot(h2g, w_gu, preferred_element_type=F32)
    gate, up = gu[:, :n_ff], gu[:, n_ff:]
    sig = jax.nn.sigmoid(gate)
    act = (gate * sig * up).astype(BF)
    d_act = lax.dot_general(dyg, w_dn, (((1,), (1,)), ((), ())), preferred_element_type=F32)
    d_gate = (d_act * up * sig * (1.0 + gate * (1.0 - sig))).astype(BF)
    d_up = (d_act * gate * sig).astype(BF)
    d_gu = jnp.concatenate([d_gate, d_up], axis=1)
    d_h2 = lax.dot_general(d_gu, w_gu, (((1,), (1,)), ((), ())), preferred_element_type=F32)
    d_h2 = scatter_group(d_h2.reshape(4, 2, count, width))
    down = jnp.dot(act, w_dn, preferred_element_type=F32)
    result = (mid + scatter_group(down.reshape(4, 2, count, width))).astype(BF)

    grad_gain_ffn = jnp.sum(d_h2 * mid_unit, axis=0)
    d_mid = grad_outputs[0].astype(F32) + rms_back(mid_unit, mid_scale, gain_ffn, d_h2)
    d_mid_low = d_mid.astype(BF)
    d_own = lax.dot_general(d_mid_low, w_out_all, (((1,), (1,)), ((), ())), preferred_element_type=F32)
    d_own = d_own.astype(BF).reshape(count, 4, 2, 2 * HD).transpose(1, 2, 0, 3)
    d_o = exchange_group(d_own).reshape(rows, 2 * HD)
    delta = jnp.sum((d_o.astype(F32) * attended).reshape(4, TILE, 2, HD), axis=-1).transpose(0, 2, 1)

    tt = (((0,), (0,)), ((), ()))
    g_gu = lax.dot_general(h2g, d_gu, tt, preferred_element_type=F32)
    g_dn = lax.dot_general(act, dyg, tt, preferred_element_type=F32)
    d_mid_g = gather_group(d_mid_low).reshape(rows, width)
    g_out = lax.dot_general(attended_low, d_mid_g, tt, preferred_element_type=F32)

    def scatter_cols(g):
        c = g.shape[1]
        g = g.reshape(4, 4, 4, 16, c)
        g = reduce_slots([g[i] for i in range(4)], Z, zi)
        g = reduce_slots([g[:, i] for i in range(4)], "x", x)
        g = g.astype(BF).reshape(8, 8, c)
        return lax.all_to_all(g, ("y", "core"), split_axis=0, concat_axis=0, tiled=True).astype(F32)

    def scatter_rows(g):
        g = g.reshape(4, 4, -1, width)
        g = reduce_slots([g[i] for i in range(4)], Z, zi)
        return reduce_slots([g[i] for i in range(4)], "x", x)

    g_gu = scatter_cols(g_gu)
    g_tall = jnp.concatenate([scatter_rows(g_out), scatter_rows(g_dn)], axis=0).astype(BF)
    g_tall = lax.ppermute(g_tall, ALL, back).astype(F32)

    dkvs = {}
    carry = None
    orders = [((1, 1), (2, 1)), ((3, 1), (0, 1)), ((1, 0), (2, 0)), ((3, 0), (0, 0))]
    for deltas in orders:
        carry, *parts = attend_back(meta, q, d_o, lse, delta, [kvs[d] for d in deltas], deltas, carry)
        dkvs.update(zip(deltas, parts))
    far = dkvs[(0, 1)].astype(F32)
    for d in (1, 2, 3):
        far = far + swap(dkvs[(d, 1)], "x", d).astype(F32)
    near = dkvs[(0, 0)].astype(F32) + swap(far.astype(BF), "head", 1).astype(F32)
    for d in (1, 2, 3):
        near = near + swap(dkvs[(d, 0)], "x", d).astype(F32)
    d_raw, gain_part = qkv_back(
        carry.astype(BF), near.astype(BF), raw, gain_query[None], gain_key[None], cos, sin
    )

    d_h1 = lax.dot_general(d_raw, w_qkv, (((1,), (1,)), ((), ())), preferred_element_type=F32)
    d_h1 = scatter_group(d_h1.reshape(4, 2, count, width))
    g_qkv = lax.dot_general(hidden, d_raw, tt, preferred_element_type=F32)
    g_qkv = scatter_cols(g_qkv)
    unit, scale = rms_parts(tokens.astype(F32))
    grad_gain_attn = jnp.sum(d_h1 * unit, axis=0)
    grad_inputs = (d_mid + rms_back(unit, scale, gain_attn, d_h1)).astype(BF)

    gains = jnp.concatenate([grad_gain_attn, grad_gain_ffn, gain_part[0], gain_part[1]])
    gains = gains + swap(gains, "core", 1)
    for axis in ("y", "x", Z):
        gains = gains + swap(gains, axis, 1) + swap(gains, axis, 2) + swap(gains, axis, 3)

    def join(g, lo, hi):
        return g[:, :, lo:hi].transpose(1, 0, 2).reshape(g.shape[1], -1)

    return (
        result[None],
        grad_inputs[None],
        join(g_qkv, 0, 2 * HD),
        join(g_qkv, 2 * HD, 3 * HD),
        join(g_qkv, 3 * HD, 4 * HD),
        g_tall[:n_out],
        join(g_gu, 0, n_ff),
        join(g_gu, n_ff, 2 * n_ff),
        g_tall[n_out:],
        gains[:width],
        gains[width : 2 * width],
        gains[2 * width : 2 * width + HD],
        gains[2 * width + HD :],
    )


def solution(mesh):
    fine = Mesh(mesh.devices.reshape(2, 2, 4, 4, 2), ALL)
    token = P("seq", ("y", "x", "core", "head"), None)
    weight = P(ALL, None)
    in_specs = (token,) + (weight,) * 7 + (P(),) * 4 + (token,)
    out_specs = (token, token) + (weight,) * 7 + (P(),) * 4
    return jax.shard_map(local, mesh=fine, in_specs=in_specs, out_specs=out_specs, check_vma=False)
```

```python
import functools

import jax
import jax.numpy as jnp
from jax import lax
from jax.experimental import pallas as pl
from jax.experimental.pallas import tpu as pltpu
from jax.sharding import Mesh, PartitionSpec as P

EPS = 1e-06
ROPE_BASE = 1000000.0
BF = jnp.bfloat16
F32 = jnp.float32
HD = 128
ALL = ("seq", "head", "y", "x", "core")
Z = ("seq", "head")
VMEM = pl.BlockSpec(memory_space=pltpu.VMEM)
ANY = pl.BlockSpec(memory_space=pl.ANY)
SMEM = pl.BlockSpec(memory_space=pltpu.SMEM)
PARAMS = pltpu.CompilerParams(vmem_limit_bytes=16 * 1024 * 1024)


def call(kernel, args, specs, shapes, out_specs, hold=(), after=(), scratch=(), cost=1.0, **rest):
    n, m, k = len(args), len(shapes), len(hold)
    skip = n + k + len(after)

    def body(*refs):
        kernel(*refs[:n], *refs[skip : skip + m], *refs[skip + m + k :])

    out = pl.pallas_call(
        body,
        in_specs=list(specs) + [ANY] * (k + len(after)),
        out_specs=list(out_specs) + [ANY] * k,
        out_shape=list(shapes) + [jax.ShapeDtypeStruct(h.shape, h.dtype) for h in hold],
        input_output_aliases={n + i: m + i for i in range(k)},
        scratch_shapes=list(scratch),
        compiler_params=PARAMS,
        cost_estimate=pl.CostEstimate(flops=int(cost * 1e9), bytes_accessed=0, transcendentals=0),
        **rest,
    )(*args, *hold, *after)
    return out[:m], out[m:]


def shape_of(*dims, dtype=BF):
    return jax.ShapeDtypeStruct(dims, dtype)


def whole_spec(a):
    return pl.BlockSpec(a.shape, lambda i: (0,) * a.ndim)


def swap(v, axis, m):
    n = 2 if axis == "core" or axis == "head" else 4
    return lax.ppermute(v, axis, [(i, i ^ m) for i in range(n)])


def stack_kernel(a, b, c, d, out):
    for i, ref in enumerate((a, b, c, d)):
        out[i] = ref[...]


def gather_group(v, after=(), hold=()):
    parts = [v] + [swap(v, "y", d) for d in (1, 2, 3)]
    (w,), held = call(
        stack_kernel, parts, [VMEM] * 4, [shape_of(4, *v.shape)], [VMEM], hold=hold, after=after, name="stack"
    )
    w = (w, swap(w, "core", 1))
    return (w, held) if hold else w


def fold_kernel(near_ref, got_ref, own_ref, s1_ref, s2_ref, s3_ref):
    i = pl.program_id(0)
    total = near_ref[0] + got_ref[0].astype(F32)

    @pl.when(i == 0)
    def _():
        own_ref[...] = total

    for d, ref in enumerate((s1_ref, s2_ref, s3_ref)):

        @pl.when(i == d + 1)
        def _(ref=ref):
            ref[...] = total.astype(BF)


def scatter_group(near, far, hold=()):
    shape = near.shape[1:]
    part = pl.BlockSpec((1,) + shape, lambda i: (i, 0, 0))
    flat = pl.BlockSpec(shape, lambda i: (0, 0))
    (own, *send), held = call(
        fold_kernel,
        [near, swap(far, "core", 1)],
        [part] * 2,
        [shape_of(*shape, dtype=F32)] + [shape_of(*shape)] * 3,
        [flat] * 4,
        hold=hold,
        grid=(4,),
        name="fold",
    )
    return [own] + [swap(send[d - 1], "y", d) for d in (1, 2, 3)], held


def trade(v, axis):
    return lax.all_to_all(v, axis, split_axis=0, concat_axis=0, tiled=True)


def copies(v):
    return jnp.broadcast_to(v[None], (16,) + v.shape)


def head_group(y, core):
    return (y & 1) * 4 + core * 2 + (y >> 1)


def place_of(j):
    return (j // 8 * 2 + j % 2) * 4 + j % 8 // 2


def pack_kernel(*refs):
    out_ref = refs[-1]
    at = 0
    for w in refs[:-1]:
        n = w.shape[1] // 8
        for p in range(8):
            b = head_group(p // 2, p % 2)
            out_ref[p, :, at : at + n] = w[:, b * n : (b + 1) * n]
        at += n


def pack(weights, after):
    cols = sum(w.shape[1] for w in weights) // 8
    shape = (8, weights[0].shape[0], cols)
    out, _ = call(
        pack_kernel,
        weights,
        [whole_spec(w) for w in weights],
        [shape_of(*shape)],
        [pl.BlockSpec(shape, lambda i: (0, 0, 0))],
        after=after,
        grid=(1,),
        name="pack",
    )
    return out[0]


def sort_kernel(n, cols, tall_ref, a_ref, f_ref):
    v = cols[...].astype(F32).reshape(-1, cols.shape[2])
    m = a_ref.shape[2]
    rows = jnp.concatenate([tall_ref[:n, :m], tall_ref[:n, m:]], axis=0)
    first = v[:, :m].astype(BF)
    for k in range(16):
        a_ref[k, :64] = first
        a_ref[k, 64:] = rows
    c = f_ref.shape[1]
    down = tall_ref[n:].astype(F32)
    tail = jnp.concatenate([down[k : k + 8, c:] for k in (0, 8, 16)], axis=1)
    f_ref[...] = jnp.concatenate([v[:, m:], down[:, :c], tail], axis=0).astype(BF)


def sort_weights(cols, tall, n):
    c = cols.shape[2] - 4 * HD
    out, _ = call(
        functools.partial(sort_kernel, n),
        [cols, tall],
        [VMEM] * 2,
        [shape_of(16, 64 + 2 * n, 4 * HD), shape_of(96, c)],
        [VMEM] * 2,
        name="sort_weights",
    )
    return out


def order_kernel(got, qkv_ref, out_ref):
    m = got.shape[2]
    n = (got.shape[1] - 64) // 2
    for z in range(4):
        for x in range(4):
            for y in range(4):
                qkv_ref[z, y, x] = got[z * 4 + x, 16 * y : 16 * y + 16]
    for j in range(16):
        out_ref[n * j : n * j + n, :m] = got[place_of(j), 64 : 64 + n]
        out_ref[n * j : n * j + n, m:] = got[place_of(j), 64 + n :]


def order_weights(got):
    m = got.shape[2]
    n = (got.shape[1] - 64) // 2
    out, _ = call(
        order_kernel,
        [got],
        [VMEM],
        [shape_of(4, 4, 4, 16, m), shape_of(16 * n, 2 * m)],
        [VMEM] * 2,
        name="order_weights",
    )
    return out[0].reshape(-1, m), out[1]


def ffn_weights_kernel(got, gu_ref, down_ref):
    n = got.shape[2] // 3
    for z in range(4):
        for x in range(4):
            for y in range(4):
                gu_ref[z, y, x] = got[z * 4 + x, 16 * y : 16 * y + 16]
    parts = []
    for j in range(16):
        low = got[place_of(j), 64:].astype(F32)
        tail = jnp.concatenate([low[24:, k : k + n] for k in (0, n, 2 * n)], axis=0)
        parts.append(jnp.concatenate([low[:24], tail], axis=1))
    down_ref[...] = jnp.concatenate(parts, axis=0).astype(BF)


def ffn_weights(got, width):
    c = got.shape[2]
    out, _ = call(
        ffn_weights_kernel,
        [got],
        [VMEM],
        [shape_of(4, 4, 4, 16, c), shape_of(c // 2, width)],
        [VMEM] * 2,
        name="ffn_weights",
    )
    return out[0].reshape(width, c), out[1]


def fold_down(down, c):
    return [down[:, :c], jnp.concatenate([down[k : k + 8, c:] for k in (0, 8, 16)], axis=1)]


def pack_ffn_kernel(gu_ref, down_ref, send_ref):
    c = send_ref.shape[3]
    for j in range(16):
        k = place_of(j)
        z, x = k // 4, k % 4
        v = [gu_ref[z, y, x] for y in range(4)] + fold_down(down_ref[j], c)
        send_ref[z, x] = jnp.concatenate(v, axis=0).astype(BF)


def pack_ffn_grads(g_gu, g_dn):
    c = g_gu.shape[1]
    out, _ = call(
        pack_ffn_kernel,
        [g_gu.reshape(4, 4, 4, 16, c), g_dn.reshape(16, -1, g_dn.shape[1])],
        [VMEM] * 2,
        [shape_of(4, 4, 96, c)],
        [VMEM],
        name="pack_ffn_grads",
    )
    return out[0]


def pick_kernel(meta_ref, got_ref, own_ref, *send_refs):
    for d, ref in enumerate((own_ref,) + send_refs):
        ref[...] = got_ref[meta_ref[2] ^ d]


def pick_x(meta, got, after):
    out, _ = call(
        pick_kernel, [meta, got], [SMEM, VMEM], [shape_of(*got.shape[1:])] * 4, [VMEM] * 4, after=after, name="pick_x"
    )
    return out


def sum_ffn_kernel(own_ref, r1_ref, r2_ref, r3_ref, gu_ref, down_ref):
    v = own_ref[...].astype(F32)
    for ref in (r1_ref, r2_ref, r3_ref):
        v = v + ref[...].astype(F32)
    gu_ref[...] = v[:64].reshape(gu_ref.shape).astype(BF)
    n = v.shape[1] // 3
    tail = jnp.concatenate([v[88:, k : k + n] for k in (0, n, 2 * n)], axis=0)
    down_ref[...] = jnp.concatenate([v[64:88], tail], axis=1)


def sum_ffn(own, got, width):
    out, _ = call(
        sum_ffn_kernel,
        [own, *got],
        [VMEM] * 4,
        [shape_of(8, 8, own.shape[1]), shape_of(24, width, dtype=F32)],
        [VMEM] * 2,
        name="sum_ffn",
    )
    return out


def high_low(v):
    high = v.astype(BF).astype(F32)
    return jnp.concatenate([high, v - high], axis=0)


def pack_qkv_kernel(g_ref, o_ref, sums_ref, gain_ref, ffn_ref, heads_ref, send_ref, tmp_ref):
    tmp_ref[...] = jnp.zeros_like(tmp_ref)
    attn = sums_ref[...] / gain_ref[...]
    for k in range(8):
        part = slice(k * HD, (k + 1) * HD)
        tmp_ref[k : k + 1, :HD] = attn[:, part]
        tmp_ref[k : k + 1, HD : 2 * HD] = ffn_ref[:, part]
    tmp_ref[0:2, 2 * HD : 3 * HD] = heads_ref[0:2, :]
    gains = high_low(tmp_ref[...])
    c = send_ref.shape[2]
    for j in range(16):
        k = place_of(j)
        v = [g_ref[k // 4, y, k % 4] for y in range(4)]
        v = v + [gains, o_ref[j, :, :c], o_ref[j, :, c:]]
        send_ref[k] = jnp.concatenate(v, axis=0).astype(BF)


def pack_qkv_grads(g_qkv, g_out, sums, gain, ffn, heads, after):
    c = g_qkv.shape[1]
    g_out = g_out.reshape(16, -1, 2 * c)
    out, _ = call(
        pack_qkv_kernel,
        [g_qkv.reshape(4, 4, 4, 16, c), g_out, sums, gain, ffn, heads],
        [VMEM] * 6,
        [shape_of(16, 80 + 2 * g_out.shape[1], c)],
        [VMEM],
        scratch=[pltpu.VMEM((8, c), F32)],
        after=after,
        name="pack_qkv_grads",
    )
    return out[0]


def total_of(ref):
    v = ref[0].astype(F32)
    for k in range(1, ref.shape[0]):
        v = v + ref[k].astype(F32)
    return v


def sum_qkv_kernel(got_ref, gu_ref, down_ref, out_ref, tall_ref):
    v = total_of(got_ref)
    n, m = v.shape[1], gu_ref.shape[2]
    out_ref[:, :, :n] = v[:64].reshape(8, 8, n).astype(BF)
    out_ref[:, :, n : n + m] = gu_ref[...]
    g = v[64:72] + v[72:80]
    high = g.astype(BF)
    low = (g - high.astype(F32)).astype(BF)
    for b in range(8):
        out_ref[b, :, n + m : 2 * n + m] = high
        out_ref[b, :, 2 * n + m :] = low
    rows = (v.shape[0] - 80) // 2
    out = jnp.concatenate([v[80 : 80 + rows], v[80 + rows :]], axis=1)
    tall_ref[...] = jnp.concatenate([out, down_ref[...]], axis=0).astype(BF)


def sum_qkv(got, gu, down, after):
    n = got.shape[2]
    rows = (got.shape[1] - 80) // 2 + down.shape[0]
    out, _ = call(
        sum_qkv_kernel,
        [got, gu, down],
        [VMEM] * 3,
        [shape_of(8, 8, 3 * n + gu.shape[2]), shape_of(rows, down.shape[1])],
        [VMEM] * 2,
        after=after,
        name="sum_qkv",
    )
    return out


def unpack_kernel(n_out, got, tall, gq, gk, gv, gg, gu, go, gd, ga, gf, gh):
    n = 4 * HD
    gains = None
    for p in range(8):
        b = head_group(p // 2, p % 2)
        total = got[p].astype(F32)
        at = 0
        for ref in (gq, gk, gv, gg, gu):
            c = ref.shape[1] // 8
            ref[:, b * c : (b + 1) * c] = total[:, at : at + c]
            at += c
        part = total[:, at : at + n] + total[:, at + n :]
        gains = part if gains is None else gains + part
    ga[...] = gains[:, :HD]
    gf[...] = gains[:, HD : 2 * HD]
    gh[...] = gains[:, 2 * HD : 3 * HD]
    go[...] = tall[:n_out].astype(F32)
    gd[...] = tall[n_out:].astype(F32)


def unpack(got, tall, n_out):
    width = tall.shape[1]
    n_ff = (got.shape[2] - 12 * HD) // 2
    cols = (16 * HD, 8 * HD, 8 * HD, 8 * n_ff, 8 * n_ff)
    shapes = [shape_of(8, c, dtype=F32) for c in cols]
    shapes += [shape_of(n_out, width, dtype=F32), shape_of(tall.shape[0] - n_out, width, dtype=F32)]
    shapes += [shape_of(8, HD, dtype=F32)] * 3
    out, _ = call(
        functools.partial(unpack_kernel, n_out), [got, tall], [VMEM] * 2, shapes, [VMEM] * len(shapes), name="unpack"
    )
    return out


def qkv_kernel(xa_ref, xb_ref, gain_ref, w_ref, gq_ref, gk_ref, cos_ref, sin_ref, h_ref, q_ref, kv_ref, raw_ref):
    n, count, _ = xa_ref.shape
    factor = HD ** (-0.5)
    for i in range(n):
        rows = slice(2 * count * i, 2 * count * (i + 1))
        x = jnp.concatenate([xa_ref[i], xb_ref[i]], axis=0).astype(F32)
        scale = lax.rsqrt(jnp.mean(x * x, axis=-1, keepdims=True) + EPS)
        h_ref[rows] = (x * scale * gain_ref[...]).astype(BF)
    for i in range(2):
        rows = slice(4 * count * i, 4 * count * (i + 1))
        raw = jnp.dot(h_ref[rows], w_ref[...], preferred_element_type=F32)
        raw_ref[rows] = raw[:, : 3 * HD]
        cos, sin = cos_ref[rows], sin_ref[rows]

        def shaped(v, gain, factor):
            r = lax.rsqrt(jnp.mean(v * v, axis=-1, keepdims=True) + EPS)
            u = v * r * gain
            return ((u * cos + pltpu.roll(u, HD // 2, 1) * sin) * factor).astype(BF)

        q_ref[rows, :HD] = shaped(raw[:, :HD], gq_ref[...], factor)
        q_ref[rows, HD:] = shaped(raw[:, HD : 2 * HD], gq_ref[...], factor)
        kv_ref[rows, :HD] = shaped(raw[:, 2 * HD : 3 * HD], gk_ref[...], 1.0)
        kv_ref[rows, HD:] = raw[:, 3 * HD :].astype(BF)


def qkv_project(xa, xb, gain, w, gq, gk, cos, sin, hold=(), after=()):
    n, count, width = xa.shape
    rows = 2 * n * count
    return call(
        qkv_kernel,
        [xa, xb, gain, w, gq, gk, cos, sin],
        [VMEM] * 8,
        [shape_of(rows, width), shape_of(rows, 2 * HD), shape_of(rows, 2 * HD), shape_of(rows, 3 * HD, dtype=F32)],
        [VMEM] * 4,
        hold=hold,
        after=after,
        name="qkv_project",
    )


def qkv_back_kernel(dq_ref, d0, d1, d2, d3, d4, raw_ref, gq_ref, gk_ref, cos_ref, sin_ref, out_ref, gain_ref):
    cos = cos_ref[...]
    sin = sin_ref[...]

    @pl.when(pl.program_id(0) == 0)
    def _():
        gain_ref[...] = jnp.zeros_like(gain_ref)

    def back(d, v, gain, factor):
        d = d.astype(BF).astype(F32) * factor
        d = d * cos + pltpu.roll(d * sin, HD // 2, 1)
        r = lax.rsqrt(jnp.mean(v * v, axis=-1, keepdims=True) + EPS)
        u = v * r
        t = d * gain
        raw = r * (t - u * jnp.mean(t * u, axis=-1, keepdims=True))
        return raw.astype(BF), jnp.sum(d * u, axis=0, keepdims=True)

    factor = HD ** (-0.5)
    dkv = d0[...].astype(F32)
    for ref in (d1, d2, d3, d4):
        dkv = dkv + ref[...].astype(F32)
    a, ga = back(dq_ref[:HD, :].T, raw_ref[:, :HD], gq_ref[...], factor)
    b, gb = back(dq_ref[HD:, :].T, raw_ref[:, HD : 2 * HD], gq_ref[...], factor)
    c, gc = back(dkv[:, :HD], raw_ref[:, 2 * HD :], gk_ref[...], 1.0)
    out_ref[:, :HD] = a
    out_ref[:, HD : 2 * HD] = b
    out_ref[:, 2 * HD : 3 * HD] = c
    out_ref[:, 3 * HD :] = dkv[:, HD:].astype(BF)
    gain_ref[0:1, :] += ga + gb
    gain_ref[1:2, :] += gc


def qkv_back(dq, dkvs, raw, gq, gk, cos, sin, after):
    rows = dq.shape[1]
    tile = 256
    row = lambda n: pl.BlockSpec((tile, n), lambda i: (i, 0))
    out, _ = call(
        qkv_back_kernel,
        [dq, *dkvs, raw, gq, gk, cos, sin],
        [pl.BlockSpec((2 * HD, tile), lambda i: (0, i))]
        + [row(2 * HD)] * 5
        + [row(3 * HD), whole_spec(gq), whole_spec(gk), row(HD), row(HD)],
        [shape_of(rows, 4 * HD), shape_of(8, HD, dtype=F32)],
        [row(4 * HD), pl.BlockSpec((8, HD), lambda i: (0, 0))],
        after=after,
        grid=(rows // tile,),
        name="qkv_back",
    )
    return out


NT = (((1,), (1,)), ((), ()))


def ffn_kernel(ha_ref, hb_ref, ya_ref, yb_ref, wgu_ref, wd_ref, act_ref, dgu_ref, near_ref, far_ref):
    n = wd_ref.shape[0]
    width = wd_ref.shape[1]
    for e, (h_ref, y_ref) in enumerate(((ha_ref, ya_ref), (hb_ref, yb_ref))):
        h = h_ref[...].reshape(-1, width)
        dy = y_ref[...].reshape(-1, width)
        gu = jnp.dot(h, wgu_ref[...], preferred_element_type=F32)
        d_act = lax.dot_general(dy, wd_ref[...], NT, preferred_element_type=F32)
        gate, up = gu[:, :n], gu[:, n:]
        sig = 1.0 / (1.0 + jnp.exp(-gate))
        silu = gate * sig
        act_ref[e] = (silu * up).astype(BF).reshape(act_ref.shape[1:])
        d_gate = (d_act * up * (sig + silu * (1.0 - sig))).astype(BF)
        d_up = (d_act * silu).astype(BF)
        d_gu = jnp.concatenate([d_gate, d_up], axis=1)
        dgu_ref[e] = d_gu.reshape(dgu_ref.shape[1:])
        d_h = lax.dot_general(d_gu, wgu_ref[...], NT, preferred_element_type=F32).reshape(near_ref.shape)
        if e == 0:
            near_ref[...] = d_h
        else:
            far_ref[...] = d_h.astype(BF)


def feed_forward(h, dy, wgu, wd):
    n, count, width = h[0].shape
    ff = wd.shape[0]
    out, _ = call(
        ffn_kernel,
        [*h, *dy, wgu, wd],
        [VMEM] * 6,
        [shape_of(2, n, count, ff), shape_of(2, n, count, 2 * ff), shape_of(n, count, width, dtype=F32), shape_of(n, count, width)],
        [VMEM] * 4,
        cost=6.0,
        name="feed_forward",
    )
    return out


def split_kernel(dims, a_ref, w_ref, near_ref, far_ref):
    a = a_ref[...].reshape(-1, a_ref.shape[-1])
    out = lax.dot_general(a, w_ref[...], dims, preferred_element_type=F32)
    count = near_ref.shape[1]
    near_ref[0] = out[:count]
    far_ref[0] = out[count:].astype(BF)


def split_product(a, spec, w, dims, n, count, width, name):
    part = pl.BlockSpec((1, count, width), lambda i: (i, 0, 0))
    out, _ = call(
        functools.partial(split_kernel, dims),
        [a, w],
        [spec, whole_spec(w)],
        [shape_of(n, count, width, dtype=F32), shape_of(n, count, width)],
        [part, part],
        grid=(n,),
        name=name,
    )
    return out


def down_kernel(meta_ref, act_ref, w_ref, out_ref):
    y, core = meta_ref[0], meta_ref[1]
    for d in range(4):
        for e in range(2):
            at = (y ^ d) * 2 + (core ^ e)
            out_ref[at] = jnp.dot(act_ref[e, d], w_ref[...], preferred_element_type=F32)


def down_project(meta, act, w):
    count = act.shape[2]
    out, _ = call(
        down_kernel,
        [meta, act, w],
        [SMEM, VMEM, VMEM],
        [shape_of(8, count, w.shape[1], dtype=F32)],
        [VMEM],
        name="down_project",
    )
    return out[0].reshape(8 * count, -1)


TN = (((0,), (0,)), ((), ()))


def rows_of(a, b):
    return jnp.concatenate([a[...].reshape(-1, a.shape[2]), b[...].reshape(-1, b.shape[2])], axis=0)


def ffn_grads_kernel(meta_ref, ha_ref, hb_ref, ya_ref, yb_ref, act_ref, dgu_ref, gu_ref, down_ref):
    h = rows_of(ha_ref, hb_ref)
    gu_ref[...] = lax.dot_general(h, dgu_ref[...], TN, preferred_element_type=F32)

    @pl.when(pl.program_id(0) < 3)
    def _():
        dy = jnp.concatenate([r[d] for r in (ya_ref, yb_ref) for d in range(4)], axis=0)
        down_ref[...] = lax.dot_general(act_ref[...], dy, TN, preferred_element_type=F32)


def ffn_grads(meta, h, dy, act, d_gu):
    n, count, width = h[0].shape
    rows = 2 * n * count
    ff = act.shape[-1]
    part = pl.BlockSpec((n, count, width // 4), lambda i: (0, 0, i))
    third = lambda i: jnp.minimum(i, 2)
    out, _ = call(
        ffn_grads_kernel,
        [meta, *h, *dy, act.reshape(rows, ff), d_gu.reshape(rows, 2 * ff)],
        [SMEM, part, part]
        + [whole_spec(dy[0])] * 2
        + [pl.BlockSpec((rows, ff // 3), lambda i: (0, third(i))), pl.BlockSpec((rows, 2 * ff), lambda i: (0, 0))],
        [shape_of(width, 2 * ff, dtype=F32), shape_of(ff, width, dtype=F32)],
        [pl.BlockSpec((width // 4, 2 * ff), lambda i: (i, 0)), pl.BlockSpec((ff // 3, width), lambda i: (third(i), 0))],
        grid=(4,),
        name="ffn_grads",
    )
    return out


def out_grads_kernel(o_ref, a_ref, b_ref, out_ref):
    n = a_ref.shape[0]
    d = jnp.concatenate([r[i] for i in range(n) for r in (a_ref, b_ref)], axis=0)
    out_ref[...] = lax.dot_general(o_ref[...], d, TN, preferred_element_type=F32)


def out_grads(o, a, b):
    n, count, width = a.shape
    part = pl.BlockSpec((n, count, width // 4), lambda i: (0, 0, i))
    out, _ = call(
        out_grads_kernel,
        [o, a, b],
        [whole_spec(o), part, part],
        [shape_of(o.shape[1], width, dtype=F32)],
        [pl.BlockSpec((o.shape[1], width // 4), lambda i: (0, i))],
        grid=(4,),
        name="out_grads",
    )
    return out[0]


def middle_kernel(x_ref, own_ref, r1_ref, r2_ref, r3_ref, gain_ref, mid_ref, h_ref):
    mid = x_ref[...].astype(F32) + own_ref[...]
    for ref in (r1_ref, r2_ref, r3_ref):
        mid = mid + ref[...].astype(F32)
    mid_ref[...] = mid
    scale = lax.rsqrt(jnp.mean(mid * mid, axis=-1, keepdims=True) + EPS)
    h_ref[...] = (mid * scale * gain_ref[...]).astype(BF)


def middle(x, parts, gain, after):
    out, _ = call(
        middle_kernel,
        [x, *parts, gain],
        [VMEM] * 6,
        [shape_of(*x.shape, dtype=F32), shape_of(*x.shape)],
        [VMEM] * 2,
        after=after,
        name="middle",
    )
    return out


def norm_back_kernel(v_ref, res_ref, gain_ref, own_ref, r1_ref, r2_ref, r3_ref, out_ref, low_ref, sum_ref):
    grad = own_ref[...] + r1_ref[...].astype(F32) + r2_ref[...].astype(F32) + r3_ref[...].astype(F32)
    v = v_ref[...].astype(F32)
    scale = lax.rsqrt(jnp.mean(v * v, axis=-1, keepdims=True) + EPS)
    unit = v * scale
    t = grad * gain_ref[...]
    out = res_ref[...].astype(F32) + scale * (t - unit * jnp.mean(t * unit, axis=-1, keepdims=True))
    out_ref[...] = out
    low_ref[...] = out.astype(BF)
    sum_ref[...] = jnp.sum(grad * unit, axis=0, keepdims=True)


def norm_back(v, residual, gain, parts, after=()):
    out, _ = call(
        norm_back_kernel,
        [v, residual, gain, *parts],
        [VMEM] * 7,
        [shape_of(*v.shape, dtype=F32), shape_of(*v.shape), shape_of(*gain.shape, dtype=F32)],
        [VMEM] * 3,
        after=after,
        name="norm_back",
    )
    return out


def heads_kernel(a_ref, b_ref, w_ref, out_ref):
    d = jnp.concatenate([a_ref[0], b_ref[0]], axis=0)
    out_ref[...] = lax.dot_general(d, w_ref[...], NT, preferred_element_type=F32).astype(BF)


def heads_back(a, b, w):
    n, count, width = a.shape
    part = pl.BlockSpec((1, count, width), lambda i: (i, 0, 0))
    out, _ = call(
        heads_kernel,
        [a, b, w],
        [part, part, whole_spec(w)],
        [shape_of(2 * n * count, w.shape[0])],
        [pl.BlockSpec((2 * count, w.shape[0]), lambda i: (i, 0))],
        grid=(n,),
        name="heads_back",
    )
    return out[0]


TILE = 256


def spread(core, key_axis):
    shape = (TILE, TILE)
    a = lax.broadcasted_iota(jnp.int32, shape, key_axis)
    b = lax.broadcasted_iota(jnp.int32, shape, 1 - key_axis)
    flip = core * 128

    def place(i):
        j = i ^ flip
        return j + (j & 128)

    return place(a) - place(b)


def row_sums(v):
    ones = jnp.ones((8, v.shape[1]), F32)
    dims = (((1,), (1,)), ((), ()))
    out = lax.dot_general(ones, v, dims, precision=lax.Precision.HIGHEST, preferred_element_type=F32)
    return out[0:1]


def attend_kernel(first, last, deltas, meta_ref, *refs):
    n = len(deltas)
    q_ref = refs[0]
    kv_refs = refs[1 : 1 + n]
    at = 1 + n
    if not first:
        acc_in, sum_in = refs[at : at + 2]
        at += 2
    if last:
        att_ref, low_ref, lse_ref = refs[at : at + 3]
        acc_ref, sum_ref, mask_ref = refs[at + 3 :]
    else:
        acc_ref, sum_ref = refs[at : at + 2]
        (mask_ref,) = refs[at + 2 :]
    if first:
        acc_ref[...] = jnp.zeros_like(acc_ref)
        sum_ref[...] = jnp.zeros_like(sum_ref)
    else:
        acc_ref[...] = acc_in[...]
        sum_ref[...] = sum_in[...]
    y, core, x, head = meta_ref[0], meta_ref[1], meta_ref[2], meta_ref[3]
    mask_ref[...] = spread(core, 1)

    def tile_rows(t):
        return pl.ds(pl.multiple_of((t ^ y) * TILE, TILE), TILE)

    both = [(slice(0, HD)), (slice(HD, 2 * HD))]
    for (dx, dh), kv_ref in zip(deltas, kv_refs):
        base = ((x - (x ^ dx)) * 4 + head - (head ^ dh)) * 128
        for u in range(4):
            key = kv_ref[tile_rows(u), :HD]
            value = kv_ref[tile_rows(u), HD:]
            places = [(tile_rows(t), lanes) for t in range(u, 4) for lanes in both]
            q = jnp.concatenate([q_ref[r, c] for r, c in places], axis=0)
            s = lax.dot_general(q, key, (((1,), (1,)), ((), ())), preferred_element_type=F32)
            p = jnp.exp(s)
            keep = mask_ref[...] <= base
            diag = [jnp.where(keep, p[h * TILE : (h + 1) * TILE], 0.0) for h in range(2)]
            p = jnp.concatenate(diag + [p[2 * TILE :]], axis=0) if u < 3 else jnp.concatenate(diag, axis=0)
            part = p[:, :HD] + p[:, HD:]
            out = jnp.dot(p.astype(BF), value, preferred_element_type=F32)
            for i, (r, c) in enumerate(places):
                sum_ref[r, c] += part[i * TILE : (i + 1) * TILE]
                acc_ref[r, c] += out[i * TILE : (i + 1) * TILE]

    if last:
        for t in range(4):
            rows = pl.ds(t * TILE, TILE)
            for h, lanes in enumerate(both):
                sums = sum_ref[rows, lanes]
                lse_ref[t, h : h + 1, :] = jnp.log(row_sums(sums))
                out = acc_ref[rows, lanes] * (1.0 / jnp.sum(sums, axis=-1, keepdims=True))
                att_ref[rows, lanes] = out
                low_ref[rows, lanes] = out.astype(BF)


def attend(meta, q, chunks, deltas, carry, last, hold=(), after=()):
    first = carry is None
    rows = q.shape[0]
    f32 = shape_of(rows, 2 * HD, dtype=F32)
    low = shape_of(rows, 2 * HD)
    lse = shape_of(4, 2, TILE, dtype=F32)
    scratch = [pltpu.VMEM((TILE, TILE), jnp.int32)]
    if last:
        scratch = [pltpu.VMEM((rows, 2 * HD), F32)] * 2 + scratch
    args = [meta, q, *chunks] + ([] if first else list(carry))
    work = len(deltas) * 10 * 512 * 256
    return call(
        functools.partial(attend_kernel, first, last, deltas),
        args,
        [SMEM] + [VMEM] * (len(args) - 1),
        [f32, low, lse] if last else [f32, f32],
        [VMEM] * (3 if last else 2),
        hold=hold,
        after=after,
        scratch=scratch,
        cost=1.8 * len(deltas),
        name="attend",
    )


def attend_back_kernel(first, deltas, meta_ref, *refs):
    n = len(deltas)
    q_ref, do_ref, lse_ref, att_ref = refs[:4]
    kv_refs = refs[4 : 4 + n]
    at = 4 + n
    if not first:
        dq_in = refs[at]
        at += 1
    dq_ref = refs[at]
    dkv_refs = refs[at + 1 : at + 1 + n]
    at += 1 + n
    if first:
        delta_ref, acc_ref, mask_ref = refs[at:]
        dq_ref[...] = jnp.zeros_like(dq_ref)
        for t in range(4):
            rows = pl.ds(t * TILE, TILE)
            for h in range(2):
                lanes = slice(h * HD, (h + 1) * HD)
                delta_ref[t, h : h + 1, :] = row_sums(do_ref[rows, lanes].astype(F32) * att_ref[rows, lanes])
    else:
        delta_ref = att_ref
        acc_ref, mask_ref = refs[at:]
        dq_ref[...] = dq_in[...]
    y, core, x, head = meta_ref[0], meta_ref[1], meta_ref[2], meta_ref[3]
    mask_ref[...] = spread(core, 0)
    nt = (((1,), (1,)), ((), ()))
    tn = (((0,), (0,)), ((), ()))

    def tile_rows(t):
        return pl.ds(pl.multiple_of((t ^ y) * TILE, TILE), TILE)

    for (dx, dh), kv_ref, dkv_ref in zip(deltas, kv_refs, dkv_refs):
        base = ((x - (x ^ dx)) * 4 + head - (head ^ dh)) * 128
        for t in range(4):
            rows = tile_rows(t)
            keys = [kv_ref[tile_rows(u), :HD] for u in range(t + 1)]
            values = [kv_ref[tile_rows(u), HD:] for u in range(t + 1)]
            key = jnp.concatenate(keys, axis=0)
            value = jnp.concatenate(values, axis=0)
            key_t = key.T
            dk = dv = None
            for h in range(2):
                lanes = slice(h * HD, (h + 1) * HD)
                q = q_ref[rows, lanes]
                do = do_ref[rows, lanes]
                s = lax.dot_general(key, q, nt, preferred_element_type=F32)
                p = jnp.exp(s - lse_ref[t ^ y, h : h + 1, :])
                tail = jnp.where(mask_ref[...] <= base, p[t * TILE :], 0.0)
                p = tail if t == 0 else jnp.concatenate([p[: t * TILE], tail], axis=0)
                dp = lax.dot_general(value, do, nt, preferred_element_type=F32)
                ds = (p * (dp - delta_ref[t ^ y, h : h + 1, :])).astype(BF)
                dv_h = jnp.dot(p.astype(BF), do, preferred_element_type=F32)
                dk_h = jnp.dot(ds, q, preferred_element_type=F32)
                dv = dv_h if dv is None else dv + dv_h
                dk = dk_h if dk is None else dk + dk_h
                dq_ref[lanes, rows] += jnp.dot(key_t, ds, preferred_element_type=F32)
            for u in range(t + 1):
                cols = tile_rows(u)
                part = slice(u * TILE, (u + 1) * TILE)
                if u == t:
                    acc_ref[cols, :HD] = dk[part]
                    acc_ref[cols, HD:] = dv[part]
                else:
                    acc_ref[cols, :HD] += dk[part]
                    acc_ref[cols, HD:] += dv[part]
        dkv_ref[...] = acc_ref[...].astype(BF)


def attend_back(meta, q, do, lse, att, chunks, deltas, carry, hold=(), after=()):
    first = carry is None
    rows = q.shape[0]
    args = [meta, q, do, lse, att, *chunks] + ([] if first else [carry])
    n = len(deltas)
    work = n * 10 * 512 * 256
    shapes = [shape_of(2 * HD, rows, dtype=F32)] + [shape_of(rows, 2 * HD)] * n
    if first:
        shapes = shapes + [shape_of(4, 2, TILE, dtype=F32)]
    return call(
        functools.partial(attend_back_kernel, first, deltas),
        args,
        [SMEM] + [VMEM] * (len(args) - 1),
        shapes,
        [VMEM] * len(shapes),
        hold=hold,
        after=after,
        scratch=[pltpu.VMEM((rows, 2 * HD), F32), pltpu.VMEM((TILE, TILE), jnp.int32)],
        cost=4.0 * len(deltas),
        name="attend_back",
    )


def local(
    inputs, w_query, key_weight, value_weight, w_output, w_gate, w_up, w_down,
    gain_attn, gain_ffn, gain_query, gain_key, grad_outputs,
):
    sq, hd = lax.axis_index("seq"), lax.axis_index("head")
    y, x, core = lax.axis_index("y"), lax.axis_index("x"), lax.axis_index("core")
    zi = sq * 2 + hd
    tokens = inputs[0]
    count, width = tokens.shape
    rows = 8 * count
    meta = jnp.stack([y, core, x, hd, zi]).astype(jnp.int32)

    slot = jnp.arange(8, dtype=jnp.int32)
    chunk = ((slot // 2) ^ y) * 16 + x * 4 + ((slot % 2) ^ core) * 2 + hd
    pos = (chunk[:, None] * count + jnp.arange(count, dtype=jnp.int32)[None, :]).reshape(-1)
    freqs = ROPE_BASE ** (-(jnp.arange(HD // 2, dtype=F32) * 2.0 / HD))
    angles = pos.astype(F32)[:, None] * freqs[None, :]
    cos, sin = jnp.cos(angles), jnp.sin(angles)
    cos = jnp.concatenate([cos, cos], axis=1)
    sin = jnp.concatenate([-sin, sin], axis=1)

    (xa, xb), (dy_own,) = gather_group(tokens, hold=(grad_outputs[0],))
    n_qkv = 4 * HD
    n_ff = w_gate.shape[1] // 8
    n_out = w_output.shape[0]
    group = ("seq", "head", "x")

    def index(s, h, yy, xx, c):
        return (((s * 2 + h) * 4 + yy) * 4 + xx) * 2 + c

    there = []
    for s in range(2):
        for h in range(2):
            for yy in range(4):
                for xx in range(4):
                    for c in range(2):
                        to = index(yy % 2, c, yy // 2 * 2 + s, xx, h)
                        there.append((index(s, h, yy, xx, c), to))
    tall = lax.ppermute(jnp.concatenate([w_output, w_down], axis=0), ALL, there)

    cols = trade(pack((w_query, key_weight, value_weight, w_gate, w_up), (tall,)), ("y", "core"))
    first, ffn = sort_weights(cols, tall, n_out)
    ffn = lax.all_gather(ffn, group, axis=0, tiled=False)
    w_qkv, w_out = order_weights(trade(first, group))
    dya, dyb = gather_group(dy_own, after=(w_qkv,))
    (hidden, q, kv, raw), _ = qkv_project(xa, xb, gain_attn[None], w_qkv, gain_query[None], gain_key[None], cos, sin)

    kv_z = swap(kv, "head", 1)
    kvs = {(0, 0): kv, (0, 1): kv_z}
    for d in (1, 3, 2):
        kvs[(d, 0)] = swap(kv, "x", d)

    def fwd(deltas, carry, last=False, hold=(), after=()):
        return attend(meta, q, [kvs[d] for d in deltas], deltas, carry, last, hold, after)

    for d in (1, 3, 2):
        kvs[(d, 1)] = swap(kv_z, "x", d)
    carry, _ = fwd(((0, 0),), None, after=(dya,))
    carry, _ = fwd(((0, 1), (1, 0), (3, 0), (2, 0)), carry, after=(dyb,))
    carry, _ = fwd(((1, 1), (3, 1), (2, 1)), carry, last=True)
    attended, attended_low, lse = carry

    near, far = split_product(
        attended_low, pl.BlockSpec((2 * count, 2 * HD), lambda i: (i, 0)), w_out, (((1,), (0,)), ((), ())),
        4, count, width, "output_project",
    )
    parts, _ = scatter_group(near, far)
    mid, h2 = middle(tokens, parts, gain_ffn[None], ())
    w_gu, w_dn = ffn_weights(ffn, width)
    ha, hb = gather_group(h2)

    act, d_gu, near, far = feed_forward((ha, hb), (dya, dyb), w_gu, w_dn)
    parts, (act, d_gu) = scatter_group(near, far, hold=(act, d_gu))
    g_gu, g_dn = ffn_grads(meta, (ha, hb), (dya, dyb), act, d_gu)
    f_send = pack_ffn_grads(g_gu, g_dn)
    d_mid, d_mid_low, grad_gain_ffn = norm_back(mid, grad_outputs[0], gain_ffn[None], parts, (f_send,))
    f_sum = lax.psum_scatter(f_send, Z, scatter_dimension=0, tiled=False)
    da, db = gather_group(d_mid_low)
    d_o = heads_back(da, db, w_out)

    dkvs = {}

    def run_back(deltas, carry, att, hold=(), after=()):
        out, held = attend_back(meta, q, d_o, lse, att, [kvs[d] for d in deltas], deltas, carry, hold, after)
        dkvs.update(zip(deltas, out[1 : 1 + len(deltas)]))
        return out, held

    (carry, *rest), (act, attended_low) = run_back(((2, 1),), None, attended, hold=(act, attended_low))
    att = rest[-1]
    down = down_project(meta, act, w_dn)
    (carry, *_), (attended_low,) = run_back(((1, 1), (3, 1)), carry, att, hold=(attended_low,), after=(down,))
    down = lax.psum_scatter(down, ("y", "core"), scatter_dimension=0, tiled=True)
    result = (mid + down).astype(BF)
    g_out = out_grads(attended_low, da, db)
    (carry, *_), _ = run_back(((0, 1), (2, 0)), carry, att, after=(g_out,))
    (carry, *_), _ = run_back(((1, 0), (3, 0)), carry, att)
    (carry, *_), _ = run_back(((0, 0),), carry, att)
    f_own, *f_send = pick_x(meta, f_sum, (carry,))
    g_gu, g_dn = sum_ffn(f_own, [swap(v, "x", d) for d, v in zip((1, 2, 3), f_send)], width)

    far = dkvs[(0, 1)].astype(F32)
    for d in (1, 2, 3):
        far = far + swap(dkvs[(d, 1)], "x", d).astype(F32)
    pieces = [dkvs[(0, 0)], swap(far.astype(BF), "head", 1)]
    pieces = pieces + [swap(dkvs[(d, 0)], "x", d) for d in (1, 2, 3)]
    d_raw, gain_part = qkv_back(carry, pieces, raw, gain_query[None], gain_key[None], cos, sin, ())

    near, far = split_product(
        d_raw, pl.BlockSpec((2 * count, n_qkv), lambda i: (i, 0)), w_qkv, NT, 4, count, width, "input_back"
    )
    g_qkv = lax.dot_general(hidden, d_raw, TN, preferred_element_type=F32)
    parts, _ = scatter_group(near, far)
    grad_inputs = norm_back(tokens, d_mid, gain_attn[None], parts)[1]

    sums = jnp.sum(g_qkv * w_qkv.astype(F32), axis=1)[None]
    grads = pack_qkv_grads(g_qkv, g_out, sums, gain_attn[None], grad_gain_ffn, gain_part, (parts[0],))
    message, g_tall = sum_qkv(trade(grads, group), g_gu, g_dn, (grad_inputs,))
    got = trade(message, ("y", "core"))
    g_tall = lax.ppermute(g_tall, ALL, there)
    g_query, g_key, g_value, g_gate, g_up, g_output, g_down, g_attn, g_ffn, g_heads = unpack(got, g_tall, n_out)

    return (
        result[None],
        grad_inputs[None],
        g_query,
        g_key,
        g_value,
        g_output,
        g_gate,
        g_up,
        g_down,
        g_attn.reshape(-1),
        g_ffn.reshape(-1),
        g_heads[0],
        g_heads[1],
    )


def solution(mesh):
    fine = Mesh(mesh.devices.reshape(2, 2, 4, 4, 2), ALL)
    token = P("seq", ("y", "x", "core", "head"), None)
    weight = P(ALL, None)
    in_specs = (token,) + (weight,) * 7 + (P(),) * 4 + (token,)
    out_specs = (token, token) + (weight,) * 7 + (P(),) * 4
    return jax.shard_map(local, mesh=fine, in_specs=in_specs, out_specs=out_specs, check_vma=False)
```

```python
import functools

import jax
import jax.numpy as jnp
from jax import lax
from jax.experimental import pallas as pl
from jax.experimental.pallas import tpu as pltpu
from jax.sharding import Mesh, PartitionSpec as P

EPS = 1e-06
ROPE_BASE = 1000000.0
BF = jnp.bfloat16
F32 = jnp.float32
HD = 128
ALL = ("seq", "head", "y", "x", "core")
Z = ("seq", "head")
VMEM = pl.BlockSpec(memory_space=pltpu.VMEM)
ANY = pl.BlockSpec(memory_space=pl.ANY)
SMEM = pl.BlockSpec(memory_space=pltpu.SMEM)


def call(kernel, args, specs, shapes, out_specs, hold=(), after=(), scratch=(), vmem=16, cost=0.0, **rest):
    n, m, k = len(args), len(shapes), len(hold)
    skip = n + k + len(after)

    def body(*refs):
        kernel(*refs[:n], *refs[skip : skip + m], *refs[skip + m + k :])

    out = pl.pallas_call(
        body,
        in_specs=list(specs) + [ANY] * (k + len(after)),
        out_specs=list(out_specs) + [ANY] * k,
        out_shape=list(shapes) + [jax.ShapeDtypeStruct(h.shape, h.dtype) for h in hold],
        input_output_aliases={n + i: m + i for i in range(k)},
        scratch_shapes=list(scratch),
        compiler_params=pltpu.CompilerParams(vmem_limit_bytes=vmem << 20),
        cost_estimate=pl.CostEstimate(flops=int(cost * 1e9) + 1, bytes_accessed=0, transcendentals=0),
        **rest,
    )(*args, *hold, *after)
    return out[:m], out[m:]


def shape_of(*dims, dtype=BF):
    return jax.ShapeDtypeStruct(dims, dtype)


def whole_spec(a):
    return pl.BlockSpec(a.shape, lambda i: (0,) * a.ndim)


def swap(v, axis, m):
    n = 2 if axis == "core" or axis == "head" else 4
    return lax.ppermute(v, axis, [(i, i ^ m) for i in range(n)])


def stack_kernel(a, b, c, d, out):
    for i, ref in enumerate((a, b, c, d)):
        out[i] = ref[...]


def gather_group(v, after=(), hold=()):
    parts = [v] + [swap(v, "y", d) for d in (1, 2, 3)]
    (w,), held = call(
        stack_kernel, parts, [VMEM] * 4, [shape_of(4, *v.shape)], [VMEM], hold=hold, after=after, name="stack"
    )
    w = (w, swap(w, "core", 1))
    return (w, held) if hold else w


def fold_kernel(near_ref, got_ref, own_ref, s1_ref, s2_ref, s3_ref):
    i = pl.program_id(0)
    total = near_ref[0] + got_ref[0].astype(F32)

    @pl.when(i == 0)
    def _():
        own_ref[...] = total

    for d, ref in enumerate((s1_ref, s2_ref, s3_ref)):

        @pl.when(i == d + 1)
        def _(ref=ref):
            ref[...] = total.astype(BF)


def scatter_group(near, far, hold=(), after=()):
    shape = near.shape[1:]
    part = pl.BlockSpec((1,) + shape, lambda i: (i, 0, 0))
    flat = pl.BlockSpec(shape, lambda i: (0, 0))
    (own, *send), held = call(
        fold_kernel,
        [near, swap(far, "core", 1)],
        [part] * 2,
        [shape_of(*shape, dtype=F32)] + [shape_of(*shape)] * 3,
        [flat] * 4,
        hold=hold,
        after=after,
        grid=(4,),
        name="fold",
    )
    return [own] + [swap(send[d - 1], "y", d) for d in (1, 2, 3)], held


def trade(v, axis):
    return lax.all_to_all(v, axis, split_axis=0, concat_axis=0, tiled=True)


def copies(v):
    return jnp.broadcast_to(v[None], (16,) + v.shape)


def head_group(y, core):
    return (y & 1) * 4 + core * 2 + (y >> 1)


def place_of(j):
    return (j // 8 * 2 + j % 2) * 4 + j % 8 // 2


def pack_kernel(*refs):
    out_ref = refs[-1]
    at = 0
    for w in refs[:-1]:
        n = w.shape[1] // 8
        for p in range(8):
            b = head_group(p // 2, p % 2)
            out_ref[p, :, at : at + n] = w[:, b * n : (b + 1) * n]
        at += n


def pack(weights, after):
    cols = sum(w.shape[1] for w in weights) // 8
    shape = (8, weights[0].shape[0], cols)
    out, _ = call(
        pack_kernel,
        weights,
        [whole_spec(w) for w in weights],
        [shape_of(*shape)],
        [pl.BlockSpec(shape, lambda i: (0, 0, 0))],
        after=after,
        vmem=60,
        grid=(1,),
        name="pack",
    )
    return out[0]


def sort_kernel(n, cols, tall_ref, a_ref, f_ref):
    v = cols[...].astype(F32).reshape(-1, cols.shape[2])
    m = a_ref.shape[2]
    rows = jnp.concatenate([tall_ref[:n, :m], tall_ref[:n, m:]], axis=0)
    first = v[:, :m].astype(BF)
    for k in range(16):
        a_ref[k, :64] = first
        a_ref[k, 64:] = rows
    c = f_ref.shape[1]
    down = tall_ref[n:].astype(F32)
    tail = jnp.concatenate([down[k : k + 8, c:] for k in (0, 8, 16)], axis=1)
    f_ref[...] = jnp.concatenate([v[:, m:], down[:, :c], tail], axis=0).astype(BF)


def sort_weights(cols, tall, n):
    c = cols.shape[2] - 4 * HD
    out, _ = call(
        functools.partial(sort_kernel, n),
        [cols, tall],
        [VMEM] * 2,
        [shape_of(16, 64 + 2 * n, 4 * HD), shape_of(96, c)],
        [VMEM] * 2,
        name="sort_weights",
    )
    return out


def order_kernel(got, qkv_ref, out_ref):
    m = got.shape[2]
    n = (got.shape[1] - 64) // 2
    for z in range(4):
        for x in range(4):
            for y in range(4):
                qkv_ref[z, y, x] = got[z * 4 + x, 16 * y : 16 * y + 16]
    for j in range(16):
        out_ref[n * j : n * j + n, :m] = got[place_of(j), 64 : 64 + n]
        out_ref[n * j : n * j + n, m:] = got[place_of(j), 64 + n :]


def order_weights(got, hold, after):
    m = got.shape[2]
    n = (got.shape[1] - 64) // 2
    out, held = call(
        order_kernel,
        [got],
        [VMEM],
        [shape_of(4, 4, 4, 16, m), shape_of(16 * n, 2 * m)],
        [VMEM] * 2,
        hold=hold,
        after=after,
        name="order_weights",
    )
    return out[0].reshape(-1, m), out[1], held


def ffn_weights_kernel(got, gu_ref, down_ref):
    n = got.shape[2] // 3
    for z in range(4):
        for x in range(4):
            for y in range(4):
                gu_ref[z, y, x] = got[z * 4 + x, 16 * y : 16 * y + 16]
    parts = []
    for j in range(16):
        low = got[place_of(j), 64:].astype(F32)
        tail = jnp.concatenate([low[24:, k : k + n] for k in (0, n, 2 * n)], axis=0)
        parts.append(jnp.concatenate([low[:24], tail], axis=1))
    down_ref[...] = jnp.concatenate(parts, axis=0).astype(BF)


def ffn_weights(got, width):
    c = got.shape[2]
    out, _ = call(
        ffn_weights_kernel,
        [got],
        [VMEM],
        [shape_of(4, 4, 4, 16, c), shape_of(c // 2, width)],
        [VMEM] * 2,
        name="ffn_weights",
    )
    return out[0].reshape(width, c), out[1]


def fold_tall(tall, c):
    q = [tall[k : k + 8, c:] for k in range(0, 40, 8)]
    zero = jnp.zeros_like(q[0])
    return [tall[:, :c], jnp.concatenate(q[:3], axis=1), jnp.concatenate(q[3:] + [zero], axis=1), jnp.zeros((8, c), F32)]


def unfold_tall(v):
    a, b = v[40:48], v[48:56]
    n = a.shape[1] // 3
    right = [a[:, :n], a[:, n : 2 * n], a[:, 2 * n :], b[:, :n], b[:, n : 2 * n]]
    return jnp.concatenate([v[:40], jnp.concatenate(right, axis=0)], axis=1)


def pack_ffn_kernel(gu_ref, out_ref, down_ref, send_ref):
    c = send_ref.shape[2]
    for j in range(16):
        k = place_of(j)
        tall = jnp.concatenate([out_ref[j], down_ref[j]], axis=0)
        v = [gu_ref[k // 4, y, k % 4] for y in range(4)] + fold_tall(tall, c)
        send_ref[k] = jnp.concatenate(v, axis=0).astype(BF)


def pack_ffn_grads(g_gu, g_out, g_dn):
    c = g_gu.shape[1]
    width = g_dn.shape[1]
    out, _ = call(
        pack_ffn_kernel,
        [g_gu.reshape(4, 4, 4, 16, c), g_out.reshape(16, -1, width), g_dn.reshape(16, -1, width)],
        [VMEM] * 3,
        [shape_of(16, 128, c)],
        [VMEM],
        cost=0.5,
        name="pack_ffn_grads",
    )
    return out[0]


def split_ffn_kernel(got_ref, gu_ref, tall_ref):
    v = got_ref[...].astype(F32)
    gu_ref[...] = v[:64].reshape(gu_ref.shape).astype(BF)
    tall_ref[...] = unfold_tall(v[64:]).astype(BF)


def split_ffn(got, width):
    out, _ = call(
        split_ffn_kernel,
        [got],
        [VMEM],
        [shape_of(8, 8, got.shape[1]), shape_of(40, width)],
        [VMEM] * 2,
        name="split_ffn",
    )
    return out


def high_low(v):
    high = v.astype(BF).astype(F32)
    return jnp.concatenate([high, v - high], axis=0)


def pack_qkv_kernel(g_ref, sums_ref, gain_ref, ffn_ref, heads_ref, send_ref, tmp_ref):
    tmp_ref[...] = jnp.zeros_like(tmp_ref)
    attn = sums_ref[...] / gain_ref[...]
    for k in range(8):
        part = slice(k * HD, (k + 1) * HD)
        tmp_ref[k : k + 1, :HD] = attn[:, part]
        tmp_ref[k : k + 1, HD : 2 * HD] = ffn_ref[:, part]
    tmp_ref[0:2, 2 * HD : 3 * HD] = heads_ref[0:2, :]
    gains = high_low(tmp_ref[...])
    for k in range(16):
        v = [g_ref[k // 4, y, k % 4] for y in range(4)] + [gains]
        send_ref[k] = jnp.concatenate(v, axis=0).astype(BF)


def pack_qkv_grads(g_qkv, sums, gain, ffn, heads, after):
    c = g_qkv.shape[1]
    out, _ = call(
        pack_qkv_kernel,
        [g_qkv.reshape(4, 4, 4, 16, c), sums, gain, ffn, heads],
        [VMEM] * 5,
        [shape_of(16, 80, c)],
        [VMEM],
        scratch=[pltpu.VMEM((8, c), F32)],
        after=after,
        name="pack_qkv_grads",
    )
    return out[0]


def total_of(ref):
    v = ref[0].astype(F32)
    for k in range(1, ref.shape[0]):
        v = v + ref[k].astype(F32)
    return v


def sum_qkv_kernel(got_ref, gu_ref, out_ref):
    v = total_of(got_ref)
    n, m = v.shape[1], gu_ref.shape[2]
    out_ref[:, :, :n] = v[:64].reshape(8, 8, n).astype(BF)
    out_ref[:, :, n : n + m] = gu_ref[...]
    g = v[64:72] + v[72:80]
    high = g.astype(BF)
    low = (g - high.astype(F32)).astype(BF)
    for b in range(8):
        out_ref[b, :, n + m : 2 * n + m] = high
        out_ref[b, :, 2 * n + m :] = low


def sum_qkv(got, gu, after):
    n = got.shape[2]
    out, _ = call(
        sum_qkv_kernel,
        [got, gu],
        [VMEM] * 2,
        [shape_of(8, 8, 3 * n + gu.shape[2])],
        [VMEM],
        after=after,
        name="sum_qkv",
    )
    return out[0]


def unpack_kernel(n_out, got, tall, gq, gk, gv, gg, gu, go, gd, ga, gf, gh):
    n = 4 * HD
    gains = None
    for p in range(8):
        b = head_group(p // 2, p % 2)
        total = got[p].astype(F32)
        at = 0
        for ref in (gq, gk, gv, gg, gu):
            c = ref.shape[1] // 8
            ref[:, b * c : (b + 1) * c] = total[:, at : at + c]
            at += c
        part = total[:, at : at + n] + total[:, at + n :]
        gains = part if gains is None else gains + part
    ga[...] = gains[:, :HD]
    gf[...] = gains[:, HD : 2 * HD]
    gh[...] = gains[:, 2 * HD : 3 * HD]
    go[...] = tall[:n_out].astype(F32)
    gd[...] = tall[n_out:].astype(F32)


def unpack(got, tall, n_out):
    width = tall.shape[1]
    n_ff = (got.shape[2] - 12 * HD) // 2
    cols = (16 * HD, 8 * HD, 8 * HD, 8 * n_ff, 8 * n_ff)
    shapes = [shape_of(8, c, dtype=F32) for c in cols]
    shapes += [shape_of(n_out, width, dtype=F32), shape_of(tall.shape[0] - n_out, width, dtype=F32)]
    shapes += [shape_of(8, HD, dtype=F32)] * 3
    out, _ = call(
        functools.partial(unpack_kernel, n_out), [got, tall], [VMEM] * 2, shapes, [VMEM] * len(shapes), name="unpack"
    )
    return out


def group_rows(meta_ref, ref, d):
    at = (meta_ref[0] ^ d) * 2
    return jnp.concatenate([ref[at + meta_ref[1]], ref[at + 1 - meta_ref[1]]], axis=0)


def qkv_kernel(meta_ref, x_ref, gain_ref, w_ref, gq_ref, gk_ref, cos_ref, sin_ref, h_ref, q_ref, kv_ref, raw_ref):
    n, count, _ = x_ref.shape
    n = n // 2
    factor = HD ** (-0.5)
    for i in range(n):
        rows = slice(2 * count * i, 2 * count * (i + 1))
        x = group_rows(meta_ref, x_ref, i).astype(F32)
        scale = lax.rsqrt(jnp.mean(x * x, axis=-1, keepdims=True) + EPS)
        h_ref[rows] = (x * scale * gain_ref[...]).astype(BF)
    for i in range(2):
        rows = slice(4 * count * i, 4 * count * (i + 1))
        raw = jnp.dot(h_ref[rows], w_ref[...], preferred_element_type=F32)
        raw_ref[rows] = raw[:, : 3 * HD]
        cos, sin = cos_ref[rows], sin_ref[rows]

        def shaped(v, gain, factor):
            r = lax.rsqrt(jnp.mean(v * v, axis=-1, keepdims=True) + EPS)
            u = v * r * gain
            return ((u * cos + pltpu.roll(u, HD // 2, 1) * sin) * factor).astype(BF)

        q_ref[rows, :HD] = shaped(raw[:, :HD], gq_ref[...], factor)
        q_ref[rows, HD:] = shaped(raw[:, HD : 2 * HD], gq_ref[...], factor)
        kv_ref[rows, :HD] = shaped(raw[:, 2 * HD : 3 * HD], gk_ref[...], 1.0)
        kv_ref[rows, HD:] = raw[:, 3 * HD :].astype(BF)


def qkv_project(meta, x, gain, w, gq, gk, cos, sin):
    n, count, width = x.shape
    rows = n * count
    out, _ = call(
        qkv_kernel,
        [meta, x, gain, w, gq, gk, cos, sin],
        [SMEM] + [VMEM] * 7,
        [shape_of(rows, width), shape_of(rows, 2 * HD), shape_of(rows, 2 * HD), shape_of(rows, 3 * HD, dtype=F32)],
        [VMEM] * 4,
        name="qkv_project",
    )
    return out


def qkv_back_kernel(dq_ref, d0, d1, d2, d3, d4, raw_ref, gq_ref, gk_ref, cos_ref, sin_ref, out_ref, gain_ref):
    cos = cos_ref[...]
    sin = sin_ref[...]

    @pl.when(pl.program_id(0) == 0)
    def _():
        gain_ref[...] = jnp.zeros_like(gain_ref)

    def back(d, v, gain, factor):
        d = d.astype(BF).astype(F32) * factor
        d = d * cos + pltpu.roll(d * sin, HD // 2, 1)
        r = lax.rsqrt(jnp.mean(v * v, axis=-1, keepdims=True) + EPS)
        u = v * r
        t = d * gain
        raw = r * (t - u * jnp.mean(t * u, axis=-1, keepdims=True))
        return raw.astype(BF), jnp.sum(d * u, axis=0, keepdims=True)

    factor = HD ** (-0.5)
    dkv = d0[...].astype(F32)
    for ref in (d1, d2, d3, d4):
        dkv = dkv + ref[...].astype(F32)
    a, ga = back(dq_ref[:HD, :].T, raw_ref[:, :HD], gq_ref[...], factor)
    b, gb = back(dq_ref[HD:, :].T, raw_ref[:, HD : 2 * HD], gq_ref[...], factor)
    c, gc = back(dkv[:, :HD], raw_ref[:, 2 * HD :], gk_ref[...], 1.0)
    out_ref[:, :HD] = a
    out_ref[:, HD : 2 * HD] = b
    out_ref[:, 2 * HD : 3 * HD] = c
    out_ref[:, 3 * HD :] = dkv[:, HD:].astype(BF)
    gain_ref[0:1, :] += ga + gb
    gain_ref[1:2, :] += gc


def qkv_back(dq, dkvs, raw, gq, gk, cos, sin, after):
    rows = dq.shape[1]
    tile = 256
    row = lambda n: pl.BlockSpec((tile, n), lambda i: (i, 0))
    out, _ = call(
        qkv_back_kernel,
        [dq, *dkvs, raw, gq, gk, cos, sin],
        [pl.BlockSpec((2 * HD, tile), lambda i: (0, i))]
        + [row(2 * HD)] * 5
        + [row(3 * HD), whole_spec(gq), whole_spec(gk), row(HD), row(HD)],
        [shape_of(rows, 4 * HD), shape_of(8, HD, dtype=F32)],
        [row(4 * HD), pl.BlockSpec((8, HD), lambda i: (0, 0))],
        after=after,
        grid=(rows // tile,),
        name="qkv_back",
    )
    return out


NT = (((1,), (1,)), ((), ()))


def core_rows(meta_ref, ref, e):
    core = meta_ref[1] ^ e
    return jnp.concatenate([ref[(meta_ref[0] ^ d) * 2 + core] for d in range(4)], axis=0)


def ffn_kernel(meta_ref, ha_ref, hb_ref, y_ref, wgu_ref, wd_ref, act_ref, dgu_ref, near_ref, far_ref):
    n = wd_ref.shape[0]
    width = wd_ref.shape[1]
    for e, h_ref in enumerate((ha_ref, hb_ref)):
        h = h_ref[...].reshape(-1, width)
        dy = core_rows(meta_ref, y_ref, e)
        gu = jnp.dot(h, wgu_ref[...], preferred_element_type=F32)
        d_act = lax.dot_general(dy, wd_ref[...], NT, preferred_element_type=F32)
        gate, up = gu[:, :n], gu[:, n:]
        sig = 1.0 / (1.0 + jnp.exp(-gate))
        silu = gate * sig
        act_ref[e] = (silu * up).astype(BF).reshape(act_ref.shape[1:])
        d_gate = (d_act * up * (sig + silu * (1.0 - sig))).astype(BF)
        d_up = (d_act * silu).astype(BF)
        d_gu = jnp.concatenate([d_gate, d_up], axis=1)
        dgu_ref[e] = d_gu.reshape(dgu_ref.shape[1:])
        d_h = lax.dot_general(d_gu, wgu_ref[...], NT, preferred_element_type=F32).reshape(near_ref.shape)
        if e == 0:
            near_ref[...] = d_h
        else:
            far_ref[...] = d_h.astype(BF)


def feed_forward(meta, h, dy, wgu, wd):
    n, count, width = h[0].shape
    ff = wd.shape[0]
    out, _ = call(
        ffn_kernel,
        [meta, *h, dy, wgu, wd],
        [SMEM] + [VMEM] * 5,
        [shape_of(2, n, count, ff), shape_of(2, n, count, 2 * ff), shape_of(n, count, width, dtype=F32), shape_of(n, count, width)],
        [VMEM] * 4,
        name="feed_forward",
    )
    return out


def split_kernel(dims, a_ref, w_ref, near_ref, far_ref):
    a = a_ref[...].reshape(-1, a_ref.shape[-1])
    out = lax.dot_general(a, w_ref[...], dims, preferred_element_type=F32)
    count = near_ref.shape[1]
    near_ref[0] = out[:count]
    far_ref[0] = out[count:].astype(BF)


def split_product(a, spec, w, dims, n, count, width, name):
    part = pl.BlockSpec((1, count, width), lambda i: (i, 0, 0))
    out, _ = call(
        functools.partial(split_kernel, dims),
        [a, w],
        [spec, whole_spec(w)],
        [shape_of(n, count, width, dtype=F32), shape_of(n, count, width)],
        [part, part],
        grid=(n,),
        name=name,
    )
    return out


TN = (((0,), (0,)), ((), ()))


def rows_of(a, b):
    return jnp.concatenate([a[...].reshape(-1, a.shape[2]), b[...].reshape(-1, b.shape[2])], axis=0)


def ffn_grads_kernel(meta_ref, ha_ref, hb_ref, y_ref, act_ref, dgu_ref, gu_ref, down_ref):
    h = rows_of(ha_ref, hb_ref)
    gu_ref[...] = lax.dot_general(h, dgu_ref[...], TN, preferred_element_type=F32)

    @pl.when(pl.program_id(0) < 3)
    def _():
        dy = jnp.concatenate([core_rows(meta_ref, y_ref, e) for e in range(2)], axis=0)
        down_ref[...] = lax.dot_general(act_ref[...], dy, TN, preferred_element_type=F32)


def ffn_grads(meta, h, dy, act, d_gu, after):
    n, count, width = h[0].shape
    rows = 2 * n * count
    ff = act.shape[-1]
    part = pl.BlockSpec((n, count, width // 4), lambda i: (0, 0, i))
    third = lambda i: jnp.minimum(i, 2)
    out, _ = call(
        ffn_grads_kernel,
        [meta, *h, dy, act.reshape(rows, ff), d_gu.reshape(rows, 2 * ff)],
        [SMEM, part, part]
        + [whole_spec(dy)]
        + [pl.BlockSpec((rows, ff // 3), lambda i: (0, third(i))), pl.BlockSpec((rows, 2 * ff), lambda i: (0, 0))],
        [shape_of(width, 2 * ff, dtype=F32), shape_of(ff, width, dtype=F32)],
        [pl.BlockSpec((width // 4, 2 * ff), lambda i: (i, 0)), pl.BlockSpec((ff // 3, width), lambda i: (third(i), 0))],
        after=after,
        grid=(4,),
        cost=6.0,
        name="ffn_grads",
    )
    return out


def out_grads_kernel(o_ref, a_ref, b_ref, out_ref):
    n = a_ref.shape[0]
    d = jnp.concatenate([r[i] for i in range(n) for r in (a_ref, b_ref)], axis=0)
    out_ref[...] = lax.dot_general(o_ref[...], d, TN, preferred_element_type=F32)


def out_grads(o, a, b):
    n, count, width = a.shape
    part = pl.BlockSpec((n, count, width // 4), lambda i: (0, 0, i))
    out, _ = call(
        out_grads_kernel,
        [o, a, b],
        [whole_spec(o), part, part],
        [shape_of(o.shape[1], width, dtype=F32)],
        [pl.BlockSpec((o.shape[1], width // 4), lambda i: (0, i))],
        grid=(4,),
        name="out_grads",
    )
    return out[0]


def middle_kernel(x_ref, own_ref, r1_ref, r2_ref, r3_ref, gain_ref, mid_ref, h_ref):
    mid = x_ref[...].astype(F32) + own_ref[...]
    for ref in (r1_ref, r2_ref, r3_ref):
        mid = mid + ref[...].astype(F32)
    mid_ref[...] = mid
    scale = lax.rsqrt(jnp.mean(mid * mid, axis=-1, keepdims=True) + EPS)
    h_ref[...] = (mid * scale * gain_ref[...]).astype(BF)


def middle(x, parts, gain, after):
    out, _ = call(
        middle_kernel,
        [x, *parts, gain],
        [VMEM] * 6,
        [shape_of(*x.shape, dtype=F32), shape_of(*x.shape)],
        [VMEM] * 2,
        after=after,
        name="middle",
    )
    return out


def result_kernel(mid_ref, own_ref, r1_ref, r2_ref, r3_ref, out_ref):
    v = mid_ref[...] + own_ref[...]
    for ref in (r1_ref, r2_ref, r3_ref):
        v = v + ref[...].astype(F32)
    out_ref[...] = v.astype(BF)


def finish_result(mid, parts, after):
    out, _ = call(result_kernel, [mid, *parts], [VMEM] * 5, [shape_of(*mid.shape)], [VMEM], after=after, name="finish_result")
    return out[0]


def sum_chunks_kernel(a, b, c, d, out):
    out[...] = (a[...].astype(F32) + b[...].astype(F32) + c[...].astype(F32) + d[...].astype(F32)).astype(BF)


def sum_chunks(parts):
    out, _ = call(
        sum_chunks_kernel, parts, [VMEM] * 4, [shape_of(*parts[0].shape)], [VMEM], name="sum_chunks"
    )
    return out[0]


def norm_back_kernel(v_ref, res_ref, gain_ref, own_ref, r1_ref, r2_ref, r3_ref, out_ref, low_ref, sum_ref):
    grad = own_ref[...] + r1_ref[...].astype(F32) + r2_ref[...].astype(F32) + r3_ref[...].astype(F32)
    v = v_ref[...].astype(F32)
    scale = lax.rsqrt(jnp.mean(v * v, axis=-1, keepdims=True) + EPS)
    unit = v * scale
    t = grad * gain_ref[...]
    out = res_ref[...].astype(F32) + scale * (t - unit * jnp.mean(t * unit, axis=-1, keepdims=True))
    out_ref[...] = out
    low_ref[...] = out.astype(BF)
    sum_ref[...] = jnp.sum(grad * unit, axis=0, keepdims=True)


def norm_back(v, residual, gain, parts, after=()):
    out, _ = call(
        norm_back_kernel,
        [v, residual, gain, *parts],
        [VMEM] * 7,
        [shape_of(*v.shape, dtype=F32), shape_of(*v.shape), shape_of(*gain.shape, dtype=F32)],
        [VMEM] * 3,
        after=after,
        name="norm_back",
    )
    return out


def heads_kernel(a_ref, b_ref, w_ref, out_ref):
    d = jnp.concatenate([a_ref[0], b_ref[0]], axis=0)
    out_ref[...] = lax.dot_general(d, w_ref[...], NT, preferred_element_type=F32).astype(BF)


def heads_back(a, b, w, after):
    n, count, width = a.shape
    part = pl.BlockSpec((1, count, width), lambda i: (i, 0, 0))
    out, _ = call(
        heads_kernel,
        [a, b, w],
        [part, part, whole_spec(w)],
        [shape_of(2 * n * count, w.shape[0])],
        [pl.BlockSpec((2 * count, w.shape[0]), lambda i: (i, 0))],
        after=after,
        grid=(n,),
        name="heads_back",
    )
    return out[0]


TILE = 256


def spread(core, key_axis):
    shape = (TILE, TILE)
    a = lax.broadcasted_iota(jnp.int32, shape, key_axis)
    b = lax.broadcasted_iota(jnp.int32, shape, 1 - key_axis)
    flip = core * 128

    def place(i):
        j = i ^ flip
        return j + (j & 128)

    return place(a) - place(b)


def row_sums(v):
    ones = jnp.ones((8, v.shape[1]), F32)
    dims = (((1,), (1,)), ((), ()))
    out = lax.dot_general(ones, v, dims, precision=lax.Precision.HIGHEST, preferred_element_type=F32)
    return out[0:1]


def attend_kernel(first, last, deltas, meta_ref, *refs):
    n = len(deltas)
    q_ref = refs[0]
    kv_refs = refs[1 : 1 + n]
    at = 1 + n
    if not first:
        acc_in, sum_in = refs[at : at + 2]
        at += 2
    if last:
        att_ref, low_ref, lse_ref = refs[at : at + 3]
        acc_ref, sum_ref, mask_ref = refs[at + 3 :]
    else:
        acc_ref, sum_ref = refs[at : at + 2]
        (mask_ref,) = refs[at + 2 :]
    if first:
        acc_ref[...] = jnp.zeros_like(acc_ref)
        sum_ref[...] = jnp.zeros_like(sum_ref)
    else:
        acc_ref[...] = acc_in[...]
        sum_ref[...] = sum_in[...]
    y, core, x, head = meta_ref[0], meta_ref[1], meta_ref[2], meta_ref[3]
    mask_ref[...] = spread(core, 1)

    def tile_rows(t):
        return pl.ds(pl.multiple_of((t ^ y) * TILE, TILE), TILE)

    both = [(slice(0, HD)), (slice(HD, 2 * HD))]
    for (dx, dh), kv_ref in zip(deltas, kv_refs):
        base = ((x - (x ^ dx)) * 4 + head - (head ^ dh)) * 128
        for u in range(4):
            key = kv_ref[tile_rows(u), :HD]
            value = kv_ref[tile_rows(u), HD:]
            places = [(tile_rows(t), lanes) for t in range(u, 4) for lanes in both]
            q = jnp.concatenate([q_ref[r, c] for r, c in places], axis=0)
            s = lax.dot_general(q, key, (((1,), (1,)), ((), ())), preferred_element_type=F32)
            p = jnp.exp(s)
            keep = mask_ref[...] <= base
            diag = [jnp.where(keep, p[h * TILE : (h + 1) * TILE], 0.0) for h in range(2)]
            p = jnp.concatenate(diag + [p[2 * TILE :]], axis=0) if u < 3 else jnp.concatenate(diag, axis=0)
            part = p[:, :HD] + p[:, HD:]
            out = jnp.dot(p.astype(BF), value, preferred_element_type=F32)
            for i, (r, c) in enumerate(places):
                sum_ref[r, c] += part[i * TILE : (i + 1) * TILE]
                acc_ref[r, c] += out[i * TILE : (i + 1) * TILE]

    if last:
        for t in range(4):
            rows = pl.ds(t * TILE, TILE)
            for h, lanes in enumerate(both):
                sums = sum_ref[rows, lanes]
                lse_ref[t, h : h + 1, :] = jnp.log(row_sums(sums))
                out = acc_ref[rows, lanes] * (1.0 / jnp.sum(sums, axis=-1, keepdims=True))
                att_ref[rows, lanes] = out
                low_ref[rows, lanes] = out.astype(BF)


def attend(meta, q, chunks, deltas, carry, last, hold=(), after=()):
    first = carry is None
    rows = q.shape[0]
    f32 = shape_of(rows, 2 * HD, dtype=F32)
    low = shape_of(rows, 2 * HD)
    lse = shape_of(4, 2, TILE, dtype=F32)
    scratch = [pltpu.VMEM((TILE, TILE), jnp.int32)]
    if last:
        scratch = [pltpu.VMEM((rows, 2 * HD), F32)] * 2 + scratch
    args = [meta, q, *chunks] + ([] if first else list(carry))
    work = len(deltas) * 10 * 512 * 256
    return call(
        functools.partial(attend_kernel, first, last, deltas),
        args,
        [SMEM] + [VMEM] * (len(args) - 1),
        [f32, low, lse] if last else [f32, f32],
        [VMEM] * (3 if last else 2),
        hold=hold,
        after=after,
        scratch=scratch,
        cost=1.8 * len(deltas),
        name="attend",
    )


def attend_back_kernel(first, deltas, meta_ref, *refs):
    n = len(deltas)
    q_ref, do_ref, lse_ref, att_ref = refs[:4]
    kv_refs = refs[4 : 4 + n]
    at = 4 + n
    if not first:
        dq_in = refs[at]
        at += 1
    dq_ref = refs[at]
    dkv_refs = refs[at + 1 : at + 1 + n]
    at += 1 + n
    if first:
        delta_ref, acc_ref, mask_ref = refs[at:]
        dq_ref[...] = jnp.zeros_like(dq_ref)
        for t in range(4):
            rows = pl.ds(t * TILE, TILE)
            for h in range(2):
                lanes = slice(h * HD, (h + 1) * HD)
                delta_ref[t, h : h + 1, :] = row_sums(do_ref[rows, lanes].astype(F32) * att_ref[rows, lanes])
    else:
        delta_ref = att_ref
        acc_ref, mask_ref = refs[at:]
        dq_ref[...] = dq_in[...]
    y, core, x, head = meta_ref[0], meta_ref[1], meta_ref[2], meta_ref[3]
    mask_ref[...] = spread(core, 0)
    nt = (((1,), (1,)), ((), ()))
    tn = (((0,), (0,)), ((), ()))

    def tile_rows(t):
        return pl.ds(pl.multiple_of((t ^ y) * TILE, TILE), TILE)

    for (dx, dh), kv_ref, dkv_ref in zip(deltas, kv_refs, dkv_refs):
        base = ((x - (x ^ dx)) * 4 + head - (head ^ dh)) * 128
        for t in range(4):
            rows = tile_rows(t)
            keys = [kv_ref[tile_rows(u), :HD] for u in range(t + 1)]
            values = [kv_ref[tile_rows(u), HD:] for u in range(t + 1)]
            key = jnp.concatenate(keys, axis=0)
            value = jnp.concatenate(values, axis=0)
            key_t = key.T
            dk = dv = None
            for h in range(2):
                lanes = slice(h * HD, (h + 1) * HD)
                q = q_ref[rows, lanes]
                do = do_ref[rows, lanes]
                s = lax.dot_general(key, q, nt, preferred_element_type=F32)
                p = jnp.exp(s - lse_ref[t ^ y, h : h + 1, :])
                tail = jnp.where(mask_ref[...] <= base, p[t * TILE :], 0.0)
                p = tail if t == 0 else jnp.concatenate([p[: t * TILE], tail], axis=0)
                dp = lax.dot_general(value, do, nt, preferred_element_type=F32)
                ds = (p * (dp - delta_ref[t ^ y, h : h + 1, :])).astype(BF)
                dv_h = jnp.dot(p.astype(BF), do, preferred_element_type=F32)
                dk_h = jnp.dot(ds, q, preferred_element_type=F32)
                dv = dv_h if dv is None else dv + dv_h
                dk = dk_h if dk is None else dk + dk_h
                dq_ref[lanes, rows] += jnp.dot(key_t, ds, preferred_element_type=F32)
            for u in range(t + 1):
                cols = tile_rows(u)
                part = slice(u * TILE, (u + 1) * TILE)
                if u == t:
                    acc_ref[cols, :HD] = dk[part]
                    acc_ref[cols, HD:] = dv[part]
                else:
                    acc_ref[cols, :HD] += dk[part]
                    acc_ref[cols, HD:] += dv[part]
        dkv_ref[...] = acc_ref[...].astype(BF)


def attend_back(meta, q, do, lse, att, chunks, deltas, carry, hold=(), after=()):
    first = carry is None
    rows = q.shape[0]
    args = [meta, q, do, lse, att, *chunks] + ([] if first else [carry])
    n = len(deltas)
    work = n * 10 * 512 * 256
    shapes = [shape_of(2 * HD, rows, dtype=F32)] + [shape_of(rows, 2 * HD)] * n
    if first:
        shapes = shapes + [shape_of(4, 2, TILE, dtype=F32)]
    return call(
        functools.partial(attend_back_kernel, first, deltas),
        args,
        [SMEM] + [VMEM] * (len(args) - 1),
        shapes,
        [VMEM] * len(shapes),
        hold=hold,
        after=after,
        scratch=[pltpu.VMEM((rows, 2 * HD), F32), pltpu.VMEM((TILE, TILE), jnp.int32)],
        cost=4.0 * len(deltas),
        name="attend_back",
    )


def local(
    inputs, w_query, key_weight, value_weight, w_output, w_gate, w_up, w_down,
    gain_attn, gain_ffn, gain_query, gain_key, grad_outputs,
):
    sq, hd = lax.axis_index("seq"), lax.axis_index("head")
    y, x, core = lax.axis_index("y"), lax.axis_index("x"), lax.axis_index("core")
    zi = sq * 2 + hd
    tokens = inputs[0]
    count, width = tokens.shape
    rows = 8 * count
    meta = jnp.stack([y, core, x, hd, zi]).astype(jnp.int32)

    slot = jnp.arange(8, dtype=jnp.int32)
    chunk = ((slot // 2) ^ y) * 16 + x * 4 + ((slot % 2) ^ core) * 2 + hd
    pos = (chunk[:, None] * count + jnp.arange(count, dtype=jnp.int32)[None, :]).reshape(-1)
    freqs = ROPE_BASE ** (-(jnp.arange(HD // 2, dtype=F32) * 2.0 / HD))
    angles = pos.astype(F32)[:, None] * freqs[None, :]
    cos, sin = jnp.cos(angles), jnp.sin(angles)
    cos = jnp.concatenate([cos, cos], axis=1)
    sin = jnp.concatenate([-sin, sin], axis=1)

    x_all = lax.all_gather(tokens, ("y", "core"), axis=0, tiled=False)
    n_qkv = 4 * HD
    n_ff = w_gate.shape[1] // 8
    n_out = w_output.shape[0]
    group = ("seq", "head", "x")

    def index(s, h, yy, xx, c):
        return (((s * 2 + h) * 4 + yy) * 4 + xx) * 2 + c

    there = []
    for s in range(2):
        for h in range(2):
            for yy in range(4):
                for xx in range(4):
                    for c in range(2):
                        to = index(yy % 2, c, yy // 2 * 2 + s, xx, h)
                        there.append((index(s, h, yy, xx, c), to))
    tall = lax.ppermute(jnp.concatenate([w_output, w_down], axis=0), ALL, there)

    cols = trade(pack((w_query, key_weight, value_weight, w_gate, w_up), (tall,)), ("y", "core"))
    first, ffn = sort_weights(cols, tall, n_out)
    ffn = lax.all_gather(lax.all_gather(ffn, "x", axis=0, tiled=False), Z, axis=0, tiled=False)
    ffn = ffn.reshape(16, 96, -1)
    w_qkv, w_out, (dy_own,) = order_weights(trade(first, group), (grad_outputs[0],), (cos, sin))
    dy_all = lax.all_gather(dy_own, ("y", "core"), axis=0, tiled=False)
    hidden, q, kv, raw = qkv_project(
        meta, x_all, gain_attn[None], w_qkv, gain_query[None], gain_key[None], cos, sin
    )

    kv_z = swap(kv, "head", 1)
    kvs = {(0, 0): kv, (0, 1): kv_z}
    for d in (1, 3, 2):
        kvs[(d, 0)] = swap(kv, "x", d)

    def fwd(deltas, carry, last=False, hold=(), after=()):
        return attend(meta, q, [kvs[d] for d in deltas], deltas, carry, last, hold, after)

    for d in (1, 3, 2):
        kvs[(d, 1)] = swap(kv_z, "x", d)
    carry, _ = fwd(((0, 0),), None)
    carry, _ = fwd(((0, 1), (1, 0), (3, 0), (2, 0)), carry)
    carry, _ = fwd(((1, 1), (3, 1), (2, 1)), carry, last=True)
    attended, attended_low, lse = carry

    near, far = split_product(
        attended_low, pl.BlockSpec((2 * count, 2 * HD), lambda i: (i, 0)), w_out, (((1,), (0,)), ((), ())),
        4, count, width, "output_project",
    )
    parts, _ = scatter_group(near, far)
    w_gu, w_dn = ffn_weights(ffn, width)
    mid, h2 = middle(tokens, parts, gain_ffn[None], (w_gu, dy_all))
    ha, hb = gather_group(h2)

    act, d_gu, near, far = feed_forward(meta, (ha, hb), dy_all, w_gu, w_dn)
    parts, (act, d_gu) = scatter_group(near, far, hold=(act, d_gu))
    g_gu, g_dn = ffn_grads(meta, (ha, hb), dy_all, act, d_gu, ())
    near, far = split_product(
        act, pl.BlockSpec((2, 1, count, n_ff), lambda i: (0, i, 0, 0)), w_dn, (((1,), (0,)), ((), ())),
        4, count, width, "down_project",
    )
    d_mid, d_mid_low, grad_gain_ffn = norm_back(mid, grad_outputs[0], gain_ffn[None], parts, (g_gu, g_dn, far))
    da, db = gather_group(d_mid_low)
    d_o = heads_back(da, db, w_out, ())
    f_send = pack_ffn_grads(g_gu, out_grads(attended_low, da, db), g_dn)
    f_sum = lax.psum_scatter(f_send.reshape(4, 4, 128, -1), Z, scatter_dimension=0, tiled=False)
    f_sum = lax.psum_scatter(f_sum, "x", scatter_dimension=0, tiled=False)

    dkvs = {}

    def run_back(deltas, carry, att, hold=(), after=()):
        out, held = attend_back(meta, q, d_o, lse, att, [kvs[d] for d in deltas], deltas, carry, hold, after)
        dkvs.update(zip(deltas, out[1 : 1 + len(deltas)]))
        return out, held

    down, _ = scatter_group(near, far, after=(d_o,))
    carry, *rest = run_back(((2, 1),), None, attended, after=(f_send, down[0]))[0]
    att = rest[-1]
    (carry, *_), _ = run_back(((1, 1), (3, 1)), carry, att)
    result = finish_result(mid, down, (carry,))
    (carry, *_), _ = run_back(((0, 1), (2, 0)), carry, att, after=(result,))
    (carry, *_), _ = run_back(((1, 0), (3, 0)), carry, att)
    far = sum_chunks([dkvs[(0, 1)]] + [swap(dkvs[(d, 1)], "x", d) for d in (1, 2, 3)])
    (carry, *_), _ = run_back(((0, 0),), carry, att, after=(far,))
    g_gu, g_tall = split_ffn(f_sum, width)
    g_tall = lax.ppermute(g_tall, ALL, there)
    pieces = [dkvs[(0, 0)], swap(far, "head", 1)]
    pieces = pieces + [swap(dkvs[(d, 0)], "x", d) for d in (1, 2, 3)]
    d_raw, gain_part = qkv_back(carry, pieces, raw, gain_query[None], gain_key[None], cos, sin, (g_gu,))

    near, far = split_product(
        d_raw, pl.BlockSpec((2 * count, n_qkv), lambda i: (i, 0)), w_qkv, NT, 4, count, width, "input_back"
    )
    g_qkv = lax.dot_general(hidden, d_raw, TN, preferred_element_type=F32)
    parts, _ = scatter_group(near, far)
    grad_inputs = norm_back(tokens, d_mid, gain_attn[None], parts)[1]

    sums = jnp.sum(g_qkv * w_qkv.astype(F32), axis=1)[None]
    grads = pack_qkv_grads(g_qkv, sums, gain_attn[None], grad_gain_ffn, gain_part, (parts[0], g_tall))
    message = sum_qkv(trade(grads, group), g_gu, (grad_inputs,))
    got = trade(message, ("y", "core"))
    g_query, g_key, g_value, g_gate, g_up, g_output, g_down, g_attn, g_ffn, g_heads = unpack(got, g_tall, n_out)

    return (
        result[None],
        grad_inputs[None],
        g_query,
        g_key,
        g_value,
        g_output,
        g_gate,
        g_up,
        g_down,
        g_attn.reshape(-1),
        g_ffn.reshape(-1),
        g_heads[0],
        g_heads[1],
    )


def solution(mesh):
    fine = Mesh(mesh.devices.reshape(2, 2, 4, 4, 2), ALL)
    token = P("seq", ("y", "x", "core", "head"), None)
    weight = P(ALL, None)
    in_specs = (token,) + (weight,) * 7 + (P(),) * 4 + (token,)
    out_specs = (token, token) + (weight,) * 7 + (P(),) * 4
    return jax.shard_map(local, mesh=fine, in_specs=in_specs, out_specs=out_specs, check_vma=False)
```

```python
import functools

import jax
import jax.numpy as jnp
from jax import lax
from jax.experimental import pallas as pl
from jax.experimental.pallas import tpu as pltpu
from jax.sharding import Mesh, PartitionSpec as P

EPS = 1e-06
ROPE_BASE = 1000000.0
BF = jnp.bfloat16
F32 = jnp.float32
HD = 128
ALL = ("seq", "head", "y", "x", "core")
Z = ("seq", "head")
VMEM = pl.BlockSpec(memory_space=pltpu.VMEM)
ANY = pl.BlockSpec(memory_space=pl.ANY)
SMEM = pl.BlockSpec(memory_space=pltpu.SMEM)


def call(kernel, args, specs, shapes, out_specs, hold=(), after=(), scratch=(), vmem=16, cost=0.0, **rest):
    n, m, k = len(args), len(shapes), len(hold)
    skip = n + k + len(after)

    def body(*refs):
        kernel(*refs[:n], *refs[skip : skip + m], *refs[skip + m + k :])

    out = pl.pallas_call(
        body,
        in_specs=list(specs) + [ANY] * (k + len(after)),
        out_specs=list(out_specs) + [ANY] * k,
        out_shape=list(shapes) + [jax.ShapeDtypeStruct(h.shape, h.dtype) for h in hold],
        input_output_aliases={n + i: m + i for i in range(k)},
        scratch_shapes=list(scratch),
        compiler_params=pltpu.CompilerParams(vmem_limit_bytes=vmem << 20),
        cost_estimate=pl.CostEstimate(flops=int(cost * 1e9) + 1, bytes_accessed=0, transcendentals=0),
        **rest,
    )(*args, *hold, *after)
    return out[:m], out[m:]


def shape_of(*dims, dtype=BF):
    return jax.ShapeDtypeStruct(dims, dtype)


def whole_spec(a):
    return pl.BlockSpec(a.shape, lambda i: (0,) * a.ndim)


def swap(v, axis, m):
    n = 2 if axis == "core" or axis == "head" else 4
    return lax.ppermute(v, axis, [(i, i ^ m) for i in range(n)])


def stack_kernel(a, b, c, d, out):
    for i, ref in enumerate((a, b, c, d)):
        out[i] = ref[...]


def gather_group(v, after=(), hold=()):
    parts = [v] + [swap(v, "y", d) for d in (1, 2, 3)]
    (w,), held = call(
        stack_kernel, parts, [VMEM] * 4, [shape_of(4, *v.shape)], [VMEM], hold=hold, after=after, name="stack"
    )
    w = (w, swap(w, "core", 1))
    return (w, held) if hold else w


def fold_kernel(near_ref, got_ref, own_ref, s1_ref, s2_ref, s3_ref):
    i = pl.program_id(0)
    total = near_ref[0] + got_ref[0].astype(F32)

    @pl.when(i == 0)
    def _():
        own_ref[...] = total

    for d, ref in enumerate((s1_ref, s2_ref, s3_ref)):

        @pl.when(i == d + 1)
        def _(ref=ref):
            ref[...] = total.astype(BF)


def scatter_group(near, far, hold=(), after=()):
    shape = near.shape[1:]
    part = pl.BlockSpec((1,) + shape, lambda i: (i, 0, 0))
    flat = pl.BlockSpec(shape, lambda i: (0, 0))
    (own, *send), held = call(
        fold_kernel,
        [near, swap(far, "core", 1)],
        [part] * 2,
        [shape_of(*shape, dtype=F32)] + [shape_of(*shape)] * 3,
        [flat] * 4,
        hold=hold,
        after=after,
        grid=(4,),
        name="fold",
    )
    return [own] + [swap(send[d - 1], "y", d) for d in (1, 2, 3)], held


def trade(v, axis):
    return lax.all_to_all(v, axis, split_axis=0, concat_axis=0, tiled=True)


def copies(v):
    return jnp.broadcast_to(v[None], (16,) + v.shape)


def head_group(y, core):
    return (y & 1) * 4 + core * 2 + (y >> 1)


def place_of(j):
    return (j // 8 * 2 + j % 2) * 4 + j % 8 // 2


def pack_kernel(*refs):
    out_ref = refs[-1]
    at = 0
    for w in refs[:-1]:
        n = w.shape[1] // 8
        for p in range(8):
            b = head_group(p // 2, p % 2)
            out_ref[p, :, at : at + n] = w[:, b * n : (b + 1) * n]
        at += n


def pack(weights, after):
    cols = sum(w.shape[1] for w in weights) // 8
    shape = (8, weights[0].shape[0], cols)
    out, _ = call(
        pack_kernel,
        weights,
        [whole_spec(w) for w in weights],
        [shape_of(*shape)],
        [pl.BlockSpec(shape, lambda i: (0, 0, 0))],
        after=after,
        vmem=60,
        grid=(1,),
        name="pack",
    )
    return out[0]


def sort_kernel(n, cols, tall_ref, a_ref, f_ref):
    v = cols[...].astype(F32).reshape(-1, cols.shape[2])
    m = a_ref.shape[2]
    rows = jnp.concatenate([tall_ref[:n, :m], tall_ref[:n, m:]], axis=0)
    first = v[:, :m].astype(BF)
    for k in range(16):
        a_ref[k, :64] = first
        a_ref[k, 64:] = rows
    c = f_ref.shape[1]
    down = tall_ref[n:].astype(F32)
    tail = jnp.concatenate([down[k : k + 8, c:] for k in (0, 8, 16)], axis=1)
    f_ref[...] = jnp.concatenate([v[:, m:], down[:, :c], tail], axis=0).astype(BF)


def sort_weights(cols, tall, n):
    c = cols.shape[2] - 4 * HD
    out, _ = call(
        functools.partial(sort_kernel, n),
        [cols, tall],
        [VMEM] * 2,
        [shape_of(16, 64 + 2 * n, 4 * HD), shape_of(96, c)],
        [VMEM] * 2,
        name="sort_weights",
    )
    return out


def order_kernel(got, qkv_ref, out_ref):
    m = got.shape[2]
    n = (got.shape[1] - 64) // 2
    for z in range(4):
        for x in range(4):
            for y in range(4):
                qkv_ref[z, y, x] = got[z * 4 + x, 16 * y : 16 * y + 16]
    for j in range(16):
        out_ref[n * j : n * j + n, :m] = got[place_of(j), 64 : 64 + n]
        out_ref[n * j : n * j + n, m:] = got[place_of(j), 64 + n :]


def order_weights(got, hold, after):
    m = got.shape[2]
    n = (got.shape[1] - 64) // 2
    out, held = call(
        order_kernel,
        [got],
        [VMEM],
        [shape_of(4, 4, 4, 16, m), shape_of(16 * n, 2 * m)],
        [VMEM] * 2,
        hold=hold,
        after=after,
        name="order_weights",
    )
    return out[0].reshape(-1, m), out[1], held


def ffn_weights_kernel(got, gu_ref, down_ref):
    n = got.shape[2] // 3
    for z in range(4):
        for x in range(4):
            for y in range(4):
                gu_ref[z, y, x] = got[z * 4 + x, 16 * y : 16 * y + 16]
    parts = []
    for j in range(16):
        low = got[place_of(j), 64:].astype(F32)
        tail = jnp.concatenate([low[24:, k : k + n] for k in (0, n, 2 * n)], axis=0)
        parts.append(jnp.concatenate([low[:24], tail], axis=1))
    down_ref[...] = jnp.concatenate(parts, axis=0).astype(BF)


def ffn_weights(got, width):
    c = got.shape[2]
    out, _ = call(
        ffn_weights_kernel,
        [got],
        [VMEM],
        [shape_of(4, 4, 4, 16, c), shape_of(c // 2, width)],
        [VMEM] * 2,
        name="ffn_weights",
    )
    return out[0].reshape(width, c), out[1]


def fold_tall(tall, c):
    q = [tall[k : k + 8, c:] for k in range(0, 40, 8)]
    zero = jnp.zeros_like(q[0])
    return [tall[:, :c], jnp.concatenate(q[:3], axis=1), jnp.concatenate(q[3:] + [zero], axis=1), jnp.zeros((8, c), F32)]


def unfold_tall(v):
    a, b = v[40:48], v[48:56]
    n = a.shape[1] // 3
    right = [a[:, :n], a[:, n : 2 * n], a[:, 2 * n :], b[:, :n], b[:, n : 2 * n]]
    return jnp.concatenate([v[:40], jnp.concatenate(right, axis=0)], axis=1)


def pack_ffn_kernel(gu_ref, out_ref, down_ref, send_ref):
    c = send_ref.shape[2]
    for j in range(16):
        k = place_of(j)
        tall = jnp.concatenate([out_ref[j], down_ref[j]], axis=0)
        v = [gu_ref[k // 4, y, k % 4] for y in range(4)] + fold_tall(tall, c)
        send_ref[k] = jnp.concatenate(v, axis=0).astype(BF)


def pack_ffn_grads(g_gu, g_out, g_dn):
    c = g_gu.shape[1]
    width = g_dn.shape[1]
    out, _ = call(
        pack_ffn_kernel,
        [g_gu.reshape(4, 4, 4, 16, c), g_out.reshape(16, -1, width), g_dn.reshape(16, -1, width)],
        [VMEM] * 3,
        [shape_of(16, 128, c)],
        [VMEM],
        cost=0.5,
        name="pack_ffn_grads",
    )
    return out[0]


def split_ffn_kernel(got_ref, gu_ref, tall_ref):
    v = got_ref[...].astype(F32)
    gu_ref[...] = v[:64].reshape(gu_ref.shape).astype(BF)
    tall_ref[...] = unfold_tall(v[64:]).astype(BF)


def split_ffn(got, width):
    out, _ = call(
        split_ffn_kernel,
        [got],
        [VMEM],
        [shape_of(8, 8, got.shape[1]), shape_of(40, width)],
        [VMEM] * 2,
        name="split_ffn",
    )
    return out


def high_low(v):
    high = v.astype(BF).astype(F32)
    return jnp.concatenate([high, v - high], axis=0)


def pack_qkv_kernel(g_ref, sums_ref, gain_ref, ffn_ref, heads_ref, send_ref, tmp_ref):
    tmp_ref[...] = jnp.zeros_like(tmp_ref)
    attn = sums_ref[...] / gain_ref[...]
    for k in range(8):
        part = slice(k * HD, (k + 1) * HD)
        tmp_ref[k : k + 1, :HD] = attn[:, part]
        tmp_ref[k : k + 1, HD : 2 * HD] = ffn_ref[:, part]
    tmp_ref[0:2, 2 * HD : 3 * HD] = heads_ref[0:2, :]
    gains = high_low(tmp_ref[...])
    for k in range(16):
        v = [g_ref[k // 4, y, k % 4] for y in range(4)] + [gains]
        send_ref[k] = jnp.concatenate(v, axis=0).astype(BF)


def pack_qkv_grads(g_qkv, sums, gain, ffn, heads, after):
    c = g_qkv.shape[1]
    out, _ = call(
        pack_qkv_kernel,
        [g_qkv.reshape(4, 4, 4, 16, c), sums, gain, ffn, heads],
        [VMEM] * 5,
        [shape_of(16, 80, c)],
        [VMEM],
        scratch=[pltpu.VMEM((8, c), F32)],
        after=after,
        name="pack_qkv_grads",
    )
    return out[0]


def total_of(ref):
    v = ref[0].astype(F32)
    for k in range(1, ref.shape[0]):
        v = v + ref[k].astype(F32)
    return v


def sum_qkv_kernel(got_ref, gu_ref, out_ref):
    v = total_of(got_ref)
    n, m = v.shape[1], gu_ref.shape[2]
    out_ref[:, :, :n] = v[:64].reshape(8, 8, n).astype(BF)
    out_ref[:, :, n : n + m] = gu_ref[...]
    g = v[64:72] + v[72:80]
    high = g.astype(BF)
    low = (g - high.astype(F32)).astype(BF)
    for b in range(8):
        out_ref[b, :, n + m : 2 * n + m] = high
        out_ref[b, :, 2 * n + m :] = low


def sum_qkv(got, gu, after):
    n = got.shape[2]
    out, _ = call(
        sum_qkv_kernel,
        [got, gu],
        [VMEM] * 2,
        [shape_of(8, 8, 3 * n + gu.shape[2])],
        [VMEM],
        after=after,
        name="sum_qkv",
    )
    return out[0]


def unpack_kernel(n_out, got, tall, gq, gk, gv, gg, gu, go, gd, ga, gf, gh):
    n = 4 * HD
    gains = None
    for p in range(8):
        b = head_group(p // 2, p % 2)
        total = got[p].astype(F32)
        at = 0
        for ref in (gq, gk, gv, gg, gu):
            c = ref.shape[1] // 8
            ref[:, b * c : (b + 1) * c] = total[:, at : at + c]
            at += c
        part = total[:, at : at + n] + total[:, at + n :]
        gains = part if gains is None else gains + part
    ga[...] = gains[:, :HD]
    gf[...] = gains[:, HD : 2 * HD]
    gh[...] = gains[:, 2 * HD : 3 * HD]
    go[...] = tall[:n_out].astype(F32)
    gd[...] = tall[n_out:].astype(F32)


def unpack(got, tall, n_out):
    width = tall.shape[1]
    n_ff = (got.shape[2] - 12 * HD) // 2
    cols = (16 * HD, 8 * HD, 8 * HD, 8 * n_ff, 8 * n_ff)
    shapes = [shape_of(8, c, dtype=F32) for c in cols]
    shapes += [shape_of(n_out, width, dtype=F32), shape_of(tall.shape[0] - n_out, width, dtype=F32)]
    shapes += [shape_of(8, HD, dtype=F32)] * 3
    out, _ = call(
        functools.partial(unpack_kernel, n_out), [got, tall], [VMEM] * 2, shapes, [VMEM] * len(shapes), name="unpack"
    )
    return out


def group_rows(meta_ref, ref, d):
    at = (meta_ref[0] ^ d) * 2
    return jnp.concatenate([ref[at + meta_ref[1]], ref[at + 1 - meta_ref[1]]], axis=0)


def qkv_kernel(meta_ref, x_ref, gain_ref, w_ref, gq_ref, gk_ref, cos_ref, sin_ref, h_ref, q_ref, kv_ref, raw_ref):
    n, count, _ = x_ref.shape
    n = n // 2
    factor = HD ** (-0.5)
    for i in range(n):
        rows = slice(2 * count * i, 2 * count * (i + 1))
        x = group_rows(meta_ref, x_ref, i).astype(F32)
        scale = lax.rsqrt(jnp.mean(x * x, axis=-1, keepdims=True) + EPS)
        h_ref[rows] = (x * scale * gain_ref[...]).astype(BF)
    for i in range(2):
        rows = slice(4 * count * i, 4 * count * (i + 1))
        raw = jnp.dot(h_ref[rows], w_ref[...], preferred_element_type=F32)
        raw_ref[rows] = raw[:, : 3 * HD]
        cos, sin = cos_ref[rows], sin_ref[rows]

        def shaped(v, gain, factor):
            r = lax.rsqrt(jnp.mean(v * v, axis=-1, keepdims=True) + EPS)
            u = v * r * gain
            return ((u * cos + pltpu.roll(u, HD // 2, 1) * sin) * factor).astype(BF)

        q_ref[rows, :HD] = shaped(raw[:, :HD], gq_ref[...], factor)
        q_ref[rows, HD:] = shaped(raw[:, HD : 2 * HD], gq_ref[...], factor)
        kv_ref[rows, :HD] = shaped(raw[:, 2 * HD : 3 * HD], gk_ref[...], 1.0)
        kv_ref[rows, HD:] = raw[:, 3 * HD :].astype(BF)


def qkv_project(meta, x, gain, w, gq, gk, cos, sin):
    n, count, width = x.shape
    rows = n * count
    out, _ = call(
        qkv_kernel,
        [meta, x, gain, w, gq, gk, cos, sin],
        [SMEM] + [VMEM] * 7,
        [shape_of(rows, width), shape_of(rows, 2 * HD), shape_of(rows, 2 * HD), shape_of(rows, 3 * HD, dtype=F32)],
        [VMEM] * 4,
        name="qkv_project",
    )
    return out


def qkv_back_kernel(dq_ref, d0, d1, d2, d3, d4, raw_ref, gq_ref, gk_ref, cos_ref, sin_ref, out_ref, gain_ref):
    cos = cos_ref[...]
    sin = sin_ref[...]

    @pl.when(pl.program_id(0) == 0)
    def _():
        gain_ref[...] = jnp.zeros_like(gain_ref)

    def back(d, v, gain, factor):
        d = d.astype(BF).astype(F32) * factor
        d = d * cos + pltpu.roll(d * sin, HD // 2, 1)
        r = lax.rsqrt(jnp.mean(v * v, axis=-1, keepdims=True) + EPS)
        u = v * r
        t = d * gain
        raw = r * (t - u * jnp.mean(t * u, axis=-1, keepdims=True))
        return raw.astype(BF), jnp.sum(d * u, axis=0, keepdims=True)

    factor = HD ** (-0.5)
    dkv = d0[...].astype(F32)
    for ref in (d1, d2, d3, d4):
        dkv = dkv + ref[...].astype(F32)
    a, ga = back(dq_ref[:HD, :].T, raw_ref[:, :HD], gq_ref[...], factor)
    b, gb = back(dq_ref[HD:, :].T, raw_ref[:, HD : 2 * HD], gq_ref[...], factor)
    c, gc = back(dkv[:, :HD], raw_ref[:, 2 * HD :], gk_ref[...], 1.0)
    out_ref[:, :HD] = a
    out_ref[:, HD : 2 * HD] = b
    out_ref[:, 2 * HD : 3 * HD] = c
    out_ref[:, 3 * HD :] = dkv[:, HD:].astype(BF)
    gain_ref[0:1, :] += ga + gb
    gain_ref[1:2, :] += gc


def qkv_back(dq, dkvs, raw, gq, gk, cos, sin, after):
    rows = dq.shape[1]
    tile = 256
    row = lambda n: pl.BlockSpec((tile, n), lambda i: (i, 0))
    out, _ = call(
        qkv_back_kernel,
        [dq, *dkvs, raw, gq, gk, cos, sin],
        [pl.BlockSpec((2 * HD, tile), lambda i: (0, i))]
        + [row(2 * HD)] * 5
        + [row(3 * HD), whole_spec(gq), whole_spec(gk), row(HD), row(HD)],
        [shape_of(rows, 4 * HD), shape_of(8, HD, dtype=F32)],
        [row(4 * HD), pl.BlockSpec((8, HD), lambda i: (0, 0))],
        after=after,
        grid=(rows // tile,),
        name="qkv_back",
    )
    return out


NT = (((1,), (1,)), ((), ()))


def core_rows(meta_ref, ref, e):
    core = meta_ref[1] ^ e
    return jnp.concatenate([ref[(meta_ref[0] ^ d) * 2 + core] for d in range(4)], axis=0)


def ffn_kernel(meta_ref, ha_ref, hb_ref, y_ref, wgu_ref, wd_ref, act_ref, dgu_ref, near_ref, far_ref):
    n = wd_ref.shape[0]
    width = wd_ref.shape[1]
    for e, h_ref in enumerate((ha_ref, hb_ref)):
        h = h_ref[...].reshape(-1, width)
        dy = core_rows(meta_ref, y_ref, e)
        gu = jnp.dot(h, wgu_ref[...], preferred_element_type=F32)
        d_act = lax.dot_general(dy, wd_ref[...], NT, preferred_element_type=F32)
        gate, up = gu[:, :n], gu[:, n:]
        sig = 1.0 / (1.0 + jnp.exp(-gate))
        silu = gate * sig
        act_ref[e] = (silu * up).astype(BF).reshape(act_ref.shape[1:])
        d_gate = (d_act * up * (sig + silu * (1.0 - sig))).astype(BF)
        d_up = (d_act * silu).astype(BF)
        d_gu = jnp.concatenate([d_gate, d_up], axis=1)
        dgu_ref[e] = d_gu.reshape(dgu_ref.shape[1:])
        d_h = lax.dot_general(d_gu, wgu_ref[...], NT, preferred_element_type=F32).reshape(near_ref.shape)
        if e == 0:
            near_ref[...] = d_h
        else:
            far_ref[...] = d_h.astype(BF)


def feed_forward(meta, h, dy, wgu, wd):
    n, count, width = h[0].shape
    ff = wd.shape[0]
    out, _ = call(
        ffn_kernel,
        [meta, *h, dy, wgu, wd],
        [SMEM] + [VMEM] * 5,
        [shape_of(2, n, count, ff), shape_of(2, n, count, 2 * ff), shape_of(n, count, width, dtype=F32), shape_of(n, count, width)],
        [VMEM] * 4,
        name="feed_forward",
    )
    return out


def split_kernel(dims, a_ref, w_ref, near_ref, far_ref):
    a = a_ref[...].reshape(-1, a_ref.shape[-1])
    out = lax.dot_general(a, w_ref[...], dims, preferred_element_type=F32)
    count = near_ref.shape[1]
    near_ref[0] = out[:count]
    far_ref[0] = out[count:].astype(BF)


def split_product(a, spec, w, dims, n, count, width, name):
    part = pl.BlockSpec((1, count, width), lambda i: (i, 0, 0))
    out, _ = call(
        functools.partial(split_kernel, dims),
        [a, w],
        [spec, whole_spec(w)],
        [shape_of(n, count, width, dtype=F32), shape_of(n, count, width)],
        [part, part],
        grid=(n,),
        name=name,
    )
    return out


TN = (((0,), (0,)), ((), ()))


def rows_of(a, b):
    return jnp.concatenate([a[...].reshape(-1, a.shape[2]), b[...].reshape(-1, b.shape[2])], axis=0)


def ffn_grads_kernel(meta_ref, ha_ref, hb_ref, y_ref, act_ref, dgu_ref, gu_ref, down_ref):
    h = rows_of(ha_ref, hb_ref)
    gu_ref[...] = lax.dot_general(h, dgu_ref[...], TN, preferred_element_type=F32)

    @pl.when(pl.program_id(0) < 3)
    def _():
        dy = jnp.concatenate([core_rows(meta_ref, y_ref, e) for e in range(2)], axis=0)
        down_ref[...] = lax.dot_general(act_ref[...], dy, TN, preferred_element_type=F32)


def ffn_grads(meta, h, dy, act, d_gu, after):
    n, count, width = h[0].shape
    rows = 2 * n * count
    ff = act.shape[-1]
    part = pl.BlockSpec((n, count, width // 4), lambda i: (0, 0, i))
    third = lambda i: jnp.minimum(i, 2)
    out, _ = call(
        ffn_grads_kernel,
        [meta, *h, dy, act.reshape(rows, ff), d_gu.reshape(rows, 2 * ff)],
        [SMEM, part, part]
        + [whole_spec(dy)]
        + [pl.BlockSpec((rows, ff // 3), lambda i: (0, third(i))), pl.BlockSpec((rows, 2 * ff), lambda i: (0, 0))],
        [shape_of(width, 2 * ff, dtype=F32), shape_of(ff, width, dtype=F32)],
        [pl.BlockSpec((width // 4, 2 * ff), lambda i: (i, 0)), pl.BlockSpec((ff // 3, width), lambda i: (third(i), 0))],
        after=after,
        grid=(4,),
        cost=6.0,
        name="ffn_grads",
    )
    return out


def out_grads_kernel(o_ref, a_ref, b_ref, out_ref):
    n = a_ref.shape[0]
    d = jnp.concatenate([r[i] for i in range(n) for r in (a_ref, b_ref)], axis=0)
    out_ref[...] = lax.dot_general(o_ref[...], d, TN, preferred_element_type=F32)


def out_grads(o, a, b):
    n, count, width = a.shape
    part = pl.BlockSpec((n, count, width // 4), lambda i: (0, 0, i))
    out, _ = call(
        out_grads_kernel,
        [o, a, b],
        [whole_spec(o), part, part],
        [shape_of(o.shape[1], width, dtype=F32)],
        [pl.BlockSpec((o.shape[1], width // 4), lambda i: (0, i))],
        grid=(4,),
        name="out_grads",
    )
    return out[0]


def middle_kernel(x_ref, own_ref, r1_ref, r2_ref, r3_ref, gain_ref, mid_ref, h_ref):
    mid = x_ref[...].astype(F32) + own_ref[...]
    for ref in (r1_ref, r2_ref, r3_ref):
        mid = mid + ref[...].astype(F32)
    mid_ref[...] = mid
    scale = lax.rsqrt(jnp.mean(mid * mid, axis=-1, keepdims=True) + EPS)
    h_ref[...] = (mid * scale * gain_ref[...]).astype(BF)


def middle(x, parts, gain, after):
    out, _ = call(
        middle_kernel,
        [x, *parts, gain],
        [VMEM] * 6,
        [shape_of(*x.shape, dtype=F32), shape_of(*x.shape)],
        [VMEM] * 2,
        after=after,
        name="middle",
    )
    return out


def result_kernel(mid_ref, own_ref, r1_ref, r2_ref, r3_ref, out_ref):
    v = mid_ref[...] + own_ref[...]
    for ref in (r1_ref, r2_ref, r3_ref):
        v = v + ref[...].astype(F32)
    out_ref[...] = v.astype(BF)


def finish_result(mid, parts, after):
    out, _ = call(result_kernel, [mid, *parts], [VMEM] * 5, [shape_of(*mid.shape)], [VMEM], after=after, name="finish_result")
    return out[0]


def sum_chunks_kernel(a, b, c, d, out):
    out[...] = (a[...].astype(F32) + b[...].astype(F32) + c[...].astype(F32) + d[...].astype(F32)).astype(BF)


def sum_chunks(parts):
    out, _ = call(
        sum_chunks_kernel, parts, [VMEM] * 4, [shape_of(*parts[0].shape)], [VMEM], name="sum_chunks"
    )
    return out[0]


def norm_back_kernel(v_ref, res_ref, gain_ref, own_ref, r1_ref, r2_ref, r3_ref, out_ref, low_ref, sum_ref):
    grad = own_ref[...] + r1_ref[...].astype(F32) + r2_ref[...].astype(F32) + r3_ref[...].astype(F32)
    v = v_ref[...].astype(F32)
    scale = lax.rsqrt(jnp.mean(v * v, axis=-1, keepdims=True) + EPS)
    unit = v * scale
    t = grad * gain_ref[...]
    out = res_ref[...].astype(F32) + scale * (t - unit * jnp.mean(t * unit, axis=-1, keepdims=True))
    out_ref[...] = out
    low_ref[...] = out.astype(BF)
    sum_ref[...] = jnp.sum(grad * unit, axis=0, keepdims=True)


def norm_back(v, residual, gain, parts, after=()):
    out, _ = call(
        norm_back_kernel,
        [v, residual, gain, *parts],
        [VMEM] * 7,
        [shape_of(*v.shape, dtype=F32), shape_of(*v.shape), shape_of(*gain.shape, dtype=F32)],
        [VMEM] * 3,
        after=after,
        name="norm_back",
    )
    return out


def heads_kernel(a_ref, b_ref, w_ref, out_ref):
    d = jnp.concatenate([a_ref[0], b_ref[0]], axis=0)
    out_ref[...] = lax.dot_general(d, w_ref[...], NT, preferred_element_type=F32).astype(BF)


def heads_back(a, b, w, after):
    n, count, width = a.shape
    part = pl.BlockSpec((1, count, width), lambda i: (i, 0, 0))
    out, _ = call(
        heads_kernel,
        [a, b, w],
        [part, part, whole_spec(w)],
        [shape_of(2 * n * count, w.shape[0])],
        [pl.BlockSpec((2 * count, w.shape[0]), lambda i: (i, 0))],
        after=after,
        grid=(n,),
        name="heads_back",
    )
    return out[0]


TILE = 256


def spread(core, key_axis):
    shape = (TILE, TILE)
    a = lax.broadcasted_iota(jnp.int32, shape, key_axis)
    b = lax.broadcasted_iota(jnp.int32, shape, 1 - key_axis)
    flip = core * 128

    def place(i):
        j = i ^ flip
        return j + (j & 128)

    return place(a) - place(b)


def row_sums(v):
    ones = jnp.ones((8, v.shape[1]), F32)
    dims = (((1,), (1,)), ((), ()))
    out = lax.dot_general(ones, v, dims, precision=lax.Precision.HIGHEST, preferred_element_type=F32)
    return out[0:1]


def attend_kernel(first, last, deltas, meta_ref, *refs):
    n = len(deltas)
    q_ref = refs[0]
    kv_refs = refs[1 : 1 + n]
    at = 1 + n
    if not first:
        acc_in, sum_in = refs[at : at + 2]
        at += 2
    if last:
        att_ref, low_ref, lse_ref = refs[at : at + 3]
        acc_ref, sum_ref, mask_ref = refs[at + 3 :]
    else:
        acc_ref, sum_ref = refs[at : at + 2]
        (mask_ref,) = refs[at + 2 :]
    if first:
        acc_ref[...] = jnp.zeros_like(acc_ref)
        sum_ref[...] = jnp.zeros_like(sum_ref)
    else:
        acc_ref[...] = acc_in[...]
        sum_ref[...] = sum_in[...]
    y, core, x, head = meta_ref[0], meta_ref[1], meta_ref[2], meta_ref[3]
    mask_ref[...] = spread(core, 1)

    def tile_rows(t):
        return pl.ds(pl.multiple_of((t ^ y) * TILE, TILE), TILE)

    both = [(slice(0, HD)), (slice(HD, 2 * HD))]
    for (dx, dh), kv_ref in zip(deltas, kv_refs):
        base = ((x - (x ^ dx)) * 4 + head - (head ^ dh)) * 128
        for u in range(4):
            key = kv_ref[tile_rows(u), :HD]
            value = kv_ref[tile_rows(u), HD:]
            places = [(tile_rows(t), lanes) for t in range(u, 4) for lanes in both]
            q = jnp.concatenate([q_ref[r, c] for r, c in places], axis=0)
            s = lax.dot_general(q, key, (((1,), (1,)), ((), ())), preferred_element_type=F32)
            p = jnp.exp(s)
            keep = mask_ref[...] <= base
            diag = [jnp.where(keep, p[h * TILE : (h + 1) * TILE], 0.0) for h in range(2)]
            p = jnp.concatenate(diag + [p[2 * TILE :]], axis=0) if u < 3 else jnp.concatenate(diag, axis=0)
            part = p[:, :HD] + p[:, HD:]
            out = jnp.dot(p.astype(BF), value, preferred_element_type=F32)
            for i, (r, c) in enumerate(places):
                sum_ref[r, c] += part[i * TILE : (i + 1) * TILE]
                acc_ref[r, c] += out[i * TILE : (i + 1) * TILE]

    if last:
        for t in range(4):
            rows = pl.ds(t * TILE, TILE)
            for h, lanes in enumerate(both):
                sums = sum_ref[rows, lanes]
                lse_ref[t, h : h + 1, :] = jnp.log(row_sums(sums))
                out = acc_ref[rows, lanes] * (1.0 / jnp.sum(sums, axis=-1, keepdims=True))
                att_ref[rows, lanes] = out
                low_ref[rows, lanes] = out.astype(BF)


def attend(meta, q, chunks, deltas, carry, last, hold=(), after=()):
    first = carry is None
    rows = q.shape[0]
    f32 = shape_of(rows, 2 * HD, dtype=F32)
    low = shape_of(rows, 2 * HD)
    lse = shape_of(4, 2, TILE, dtype=F32)
    scratch = [pltpu.VMEM((TILE, TILE), jnp.int32)]
    if last:
        scratch = [pltpu.VMEM((rows, 2 * HD), F32)] * 2 + scratch
    args = [meta, q, *chunks] + ([] if first else list(carry))
    work = len(deltas) * 10 * 512 * 256
    return call(
        functools.partial(attend_kernel, first, last, deltas),
        args,
        [SMEM] + [VMEM] * (len(args) - 1),
        [f32, low, lse] if last else [f32, f32],
        [VMEM] * (3 if last else 2),
        hold=hold,
        after=after,
        scratch=scratch,
        cost=1.8 * len(deltas),
        name="attend",
    )


def attend_back_kernel(first, deltas, meta_ref, *refs):
    n = len(deltas)
    q_ref, do_ref, lse_ref, att_ref = refs[:4]
    kv_refs = refs[4 : 4 + n]
    at = 4 + n
    if not first:
        dq_in = refs[at]
        at += 1
    dq_ref = refs[at]
    dkv_refs = refs[at + 1 : at + 1 + n]
    at += 1 + n
    if first:
        delta_ref, acc_ref, mask_ref = refs[at:]
        dq_ref[...] = jnp.zeros_like(dq_ref)
        for t in range(4):
            rows = pl.ds(t * TILE, TILE)
            for h in range(2):
                lanes = slice(h * HD, (h + 1) * HD)
                delta_ref[t, h : h + 1, :] = row_sums(do_ref[rows, lanes].astype(F32) * att_ref[rows, lanes])
    else:
        delta_ref = att_ref
        acc_ref, mask_ref = refs[at:]
        dq_ref[...] = dq_in[...]
    y, core, x, head = meta_ref[0], meta_ref[1], meta_ref[2], meta_ref[3]
    mask_ref[...] = spread(core, 0)
    nt = (((1,), (1,)), ((), ()))
    tn = (((0,), (0,)), ((), ()))

    def tile_rows(t):
        return pl.ds(pl.multiple_of((t ^ y) * TILE, TILE), TILE)

    for (dx, dh), kv_ref, dkv_ref in zip(deltas, kv_refs, dkv_refs):
        base = ((x - (x ^ dx)) * 4 + head - (head ^ dh)) * 128
        for t in range(4):
            rows = tile_rows(t)
            keys = [kv_ref[tile_rows(u), :HD] for u in range(t + 1)]
            values = [kv_ref[tile_rows(u), HD:] for u in range(t + 1)]
            key = jnp.concatenate(keys, axis=0)
            value = jnp.concatenate(values, axis=0)
            key_t = key.T
            dk = dv = None
            for h in range(2):
                lanes = slice(h * HD, (h + 1) * HD)
                q = q_ref[rows, lanes]
                do = do_ref[rows, lanes]
                s = lax.dot_general(key, q, nt, preferred_element_type=F32)
                p = jnp.exp(s - lse_ref[t ^ y, h : h + 1, :])
                tail = jnp.where(mask_ref[...] <= base, p[t * TILE :], 0.0)
                p = tail if t == 0 else jnp.concatenate([p[: t * TILE], tail], axis=0)
                dp = lax.dot_general(value, do, nt, preferred_element_type=F32)
                ds = (p * (dp - delta_ref[t ^ y, h : h + 1, :])).astype(BF)
                dv_h = jnp.dot(p.astype(BF), do, preferred_element_type=F32)
                dk_h = jnp.dot(ds, q, preferred_element_type=F32)
                dv = dv_h if dv is None else dv + dv_h
                dk = dk_h if dk is None else dk + dk_h
                dq_ref[lanes, rows] += jnp.dot(key_t, ds, preferred_element_type=F32)
            for u in range(t + 1):
                cols = tile_rows(u)
                part = slice(u * TILE, (u + 1) * TILE)
                if u == t:
                    acc_ref[cols, :HD] = dk[part]
                    acc_ref[cols, HD:] = dv[part]
                else:
                    acc_ref[cols, :HD] += dk[part]
                    acc_ref[cols, HD:] += dv[part]
        dkv_ref[...] = acc_ref[...].astype(BF)


def attend_back(meta, q, do, lse, att, chunks, deltas, carry, hold=(), after=(), cost=4.0):
    first = carry is None
    rows = q.shape[0]
    args = [meta, q, do, lse, att, *chunks] + ([] if first else [carry])
    n = len(deltas)
    work = n * 10 * 512 * 256
    shapes = [shape_of(2 * HD, rows, dtype=F32)] + [shape_of(rows, 2 * HD)] * n
    if first:
        shapes = shapes + [shape_of(4, 2, TILE, dtype=F32)]
    return call(
        functools.partial(attend_back_kernel, first, deltas),
        args,
        [SMEM] + [VMEM] * (len(args) - 1),
        shapes,
        [VMEM] * len(shapes),
        hold=hold,
        after=after,
        scratch=[pltpu.VMEM((rows, 2 * HD), F32), pltpu.VMEM((TILE, TILE), jnp.int32)],
        cost=cost * len(deltas),
        name="attend_back",
    )


def local(
    inputs, w_query, key_weight, value_weight, w_output, w_gate, w_up, w_down,
    gain_attn, gain_ffn, gain_query, gain_key, grad_outputs,
):
    sq, hd = lax.axis_index("seq"), lax.axis_index("head")
    y, x, core = lax.axis_index("y"), lax.axis_index("x"), lax.axis_index("core")
    zi = sq * 2 + hd
    tokens = inputs[0]
    count, width = tokens.shape
    rows = 8 * count
    meta = jnp.stack([y, core, x, hd, zi]).astype(jnp.int32)

    slot = jnp.arange(8, dtype=jnp.int32)
    chunk = ((slot // 2) ^ y) * 16 + x * 4 + ((slot % 2) ^ core) * 2 + hd
    pos = (chunk[:, None] * count + jnp.arange(count, dtype=jnp.int32)[None, :]).reshape(-1)
    freqs = ROPE_BASE ** (-(jnp.arange(HD // 2, dtype=F32) * 2.0 / HD))
    angles = pos.astype(F32)[:, None] * freqs[None, :]
    cos, sin = jnp.cos(angles), jnp.sin(angles)
    cos = jnp.concatenate([cos, cos], axis=1)
    sin = jnp.concatenate([-sin, sin], axis=1)

    x_all = lax.all_gather(tokens, ("y", "core"), axis=0, tiled=False)
    n_qkv = 4 * HD
    n_ff = w_gate.shape[1] // 8
    n_out = w_output.shape[0]
    group = ("seq", "head", "x")

    def index(s, h, yy, xx, c):
        return (((s * 2 + h) * 4 + yy) * 4 + xx) * 2 + c

    there = []
    for s in range(2):
        for h in range(2):
            for yy in range(4):
                for xx in range(4):
                    for c in range(2):
                        to = index(yy % 2, c, yy // 2 * 2 + s, xx, h)
                        there.append((index(s, h, yy, xx, c), to))
    tall = lax.ppermute(jnp.concatenate([w_output, w_down], axis=0), ALL, there)

    cols = trade(pack((w_query, key_weight, value_weight, w_gate, w_up), ()), ("y", "core"))
    first, ffn = sort_weights(cols, tall, n_out)
    ffn = lax.all_gather(lax.all_gather(ffn, "x", axis=0, tiled=False), Z, axis=0, tiled=False)
    ffn = ffn.reshape(16, 96, -1)
    w_qkv, w_out, (dy_own,) = order_weights(trade(first, group), (grad_outputs[0],), (cos, sin))
    dy_all = lax.all_gather(dy_own, ("y", "core"), axis=0, tiled=False)
    hidden, q, kv, raw = qkv_project(
        meta, x_all, gain_attn[None], w_qkv, gain_query[None], gain_key[None], cos, sin
    )

    kv_z = swap(kv, "head", 1)
    kvs = {(0, 0): kv, (0, 1): kv_z}
    for d in (1, 3, 2):
        kvs[(d, 0)] = swap(kv, "x", d)

    def fwd(deltas, carry, last=False, hold=(), after=()):
        return attend(meta, q, [kvs[d] for d in deltas], deltas, carry, last, hold, after)

    for d in (1, 3, 2):
        kvs[(d, 1)] = swap(kv_z, "x", d)
    carry, _ = fwd(((0, 0),), None)
    carry, _ = fwd(((0, 1), (1, 0), (3, 0), (2, 0)), carry)
    carry, _ = fwd(((1, 1), (3, 1), (2, 1)), carry, last=True)
    attended, attended_low, lse = carry

    near, far = split_product(
        attended_low, pl.BlockSpec((2 * count, 2 * HD), lambda i: (i, 0)), w_out, (((1,), (0,)), ((), ())),
        4, count, width, "output_project",
    )
    parts, _ = scatter_group(near, far)
    w_gu, w_dn = ffn_weights(ffn, width)
    mid, h2 = middle(tokens, parts, gain_ffn[None], (w_gu, dy_all))
    ha, hb = gather_group(h2)

    act, d_gu, near, far = feed_forward(meta, (ha, hb), dy_all, w_gu, w_dn)
    parts, (act, d_gu) = scatter_group(near, far, hold=(act, d_gu))
    g_gu, g_dn = ffn_grads(meta, (ha, hb), dy_all, act, d_gu, ())
    near, far = split_product(
        act, pl.BlockSpec((2, 1, count, n_ff), lambda i: (0, i, 0, 0)), w_dn, (((1,), (0,)), ((), ())),
        4, count, width, "down_project",
    )
    d_mid, d_mid_low, grad_gain_ffn = norm_back(mid, grad_outputs[0], gain_ffn[None], parts, (g_gu, g_dn, far))
    da, db = gather_group(d_mid_low)
    d_o = heads_back(da, db, w_out, ())
    f_send = pack_ffn_grads(g_gu, out_grads(attended_low, da, db), g_dn)
    f_sum = lax.psum_scatter(f_send.reshape(4, 4, 128, -1), Z, scatter_dimension=0, tiled=False)
    f_sum = lax.psum_scatter(f_sum, "x", scatter_dimension=0, tiled=False)

    dkvs = {}

    def run_back(deltas, carry, att, hold=(), after=(), cost=4.0):
        out, held = attend_back(meta, q, d_o, lse, att, [kvs[d] for d in deltas], deltas, carry, hold, after, cost)
        dkvs.update(zip(deltas, out[1 : 1 + len(deltas)]))
        return out, held

    down, _ = scatter_group(near, far, after=(d_o,))
    carry, *rest = run_back(((2, 1),), None, attended, after=(f_send, down[0]))[0]
    att = rest[-1]
    (carry, *_), _ = run_back(((1, 1), (3, 1)), carry, att)
    result = finish_result(mid, down, (carry,))
    (carry, *_), _ = run_back(((0, 1), (2, 0)), carry, att, after=(result,))
    far = sum_chunks([dkvs[(0, 1)]] + [swap(dkvs[(d, 1)], "x", d) for d in (1, 2, 3)])
    (carry, *_), _ = run_back(((1, 0), (3, 0)), carry, att, after=(far,), cost=12.0)
    (carry, *_), _ = run_back(((0, 0),), carry, att)
    g_gu, g_tall = split_ffn(f_sum, width)
    g_tall = lax.ppermute(g_tall, ALL, there)
    pieces = [dkvs[(0, 0)], swap(far, "head", 1)]
    pieces = pieces + [swap(dkvs[(d, 0)], "x", d) for d in (1, 2, 3)]
    d_raw, gain_part = qkv_back(carry, pieces, raw, gain_query[None], gain_key[None], cos, sin, (g_gu,))

    near, far = split_product(
        d_raw, pl.BlockSpec((2 * count, n_qkv), lambda i: (i, 0)), w_qkv, NT, 4, count, width, "input_back"
    )
    g_qkv = lax.dot_general(hidden, d_raw, TN, preferred_element_type=F32)
    parts, _ = scatter_group(near, far)
    grad_inputs = norm_back(tokens, d_mid, gain_attn[None], parts)[1]

    sums = jnp.sum(g_qkv * w_qkv.astype(F32), axis=1)[None]
    grads = pack_qkv_grads(g_qkv, sums, gain_attn[None], grad_gain_ffn, gain_part, (parts[0], g_tall))
    message = sum_qkv(trade(grads, group), g_gu, (grad_inputs,))
    got = trade(message, ("y", "core"))
    g_query, g_key, g_value, g_gate, g_up, g_output, g_down, g_attn, g_ffn, g_heads = unpack(got, g_tall, n_out)

    return (
        result[None],
        grad_inputs[None],
        g_query,
        g_key,
        g_value,
        g_output,
        g_gate,
        g_up,
        g_down,
        g_attn.reshape(-1),
        g_ffn.reshape(-1),
        g_heads[0],
        g_heads[1],
    )


def solution(mesh):
    fine = Mesh(mesh.devices.reshape(2, 2, 4, 4, 2), ALL)
    token = P("seq", ("y", "x", "core", "head"), None)
    weight = P(ALL, None)
    in_specs = (token,) + (weight,) * 7 + (P(),) * 4 + (token,)
    out_specs = (token, token) + (weight,) * 7 + (P(),) * 4
    return jax.shard_map(local, mesh=fine, in_specs=in_specs, out_specs=out_specs, check_vma=False)
```
